32 devices in a mesh: row: 4 (over x, core), col: 8 (over z, y).
Axes of the slice: x: 2, y: 2, z: 4, core: 2. Of those that a mesh axis runs over, the one named last changes fastest.
Arguments:
- currents: float32 [8192, 256], P(('row', 'col')), may hold values from -6 to 6
- branch_owner: int32 [8192, 2], P(('row', 'col')), may hold values from 0 to 31, all different within a row; in each aligned block of 256 rows (0 to 255, 256 to 511, ...) at most 64 rows name the same one
- branch_slot: int32 [8192, 2], P(('row', 'col')), may hold values from 0 to 4095
- history: bfloat16 [4, 131072, 256], P(None, 'col'), may hold values from -6 to 6
- coefficients: bfloat16 [4096, 131072], P('row', 'col'), may hold values from -0.0234375 to 0.0234375
- delays: int32 [16, 512], P('row', 'col'), may hold values from 0 to 4
- slab_owner: int32 [8192, 2], P(('row', 'col')), may hold values from 0 to 31, all different within a row; in each aligned block of 256 rows (0 to 255, 256 to 511, ...) at most 64 rows name the same one
- slab_offset: int32 [8192, 2], P(('row', 'col')), may hold values from 0 to 127
Outputs:
- charge_now: bfloat16 [131072, 256], P('col')
- drops: float32 [8192, 256], P(('row', 'col'))
The draws below stay inside these ranges and needn't reach their ends.
Inputs may be any that keep to these rules, and one draw needn't show every extreme that they name: `branch_owner`: the two ends of a branch have different owners; among the rows of one device no owner is named more than 64 times. `slab_owner`: the two ends of a slab branch have different owners; among the rows of one device no owner is named more than 64 times.
All inputs are finite; a program needn't handle non-finite values.
Results may differ from the reference program's by a relative error of at most 0.0015.
Values may be sent and summed in bfloat16 or wider, within the bound.
No kernel may reach another device: no remote copies, remote signals or barrier semaphores. Data moves between devices by JAX's collectives and lax.ppermute only.
A program may use at most 256 MiB of HBM per device.

```python
import math
import jax
import jax.numpy as jnp
import numpy as np
from jax import lax

NODES = 131072
SLAB = 4096
BLK = 256
HIST = 4
EXC = 256
BR_DEV = 256
BRANCHES = 8192
CAP = 64
OWN = 4096
SLAB_BR = 8192
SHARE = 128
SCAP = 64
DEVICES = 32


def set_ends(entries, rng, least, largest):
    shape = entries.shape
    spot = [jax.random.randint(jax.random.fold_in(rng, axis), (), 0, shape[axis]) for axis in range(len(shape))]
    entries = entries.at[tuple(spot)].set(least)
    longest = shape.index(max(shape))
    spot[longest] = (spot[longest] + 1) % shape[longest]
    return entries.at[tuple(spot)].set(largest)


def with_spikes(entries, stream_key, source, target, parts, factor):
    def block_of(position):
        return (jnp.arange(entries.shape[position]) // (entries.shape[position] // parts)).reshape((-1,) + (1,) * (entries.ndim - 1 - position))

    near = jax.random.permutation(stream_key, parts)[block_of(target)]
    far = (block_of(target) + parts // 2) % parts
    return jnp.where((block_of(source) == near) | (block_of(source) == far), factor * entries, entries)


def level_of(rng, dims, shards, smallest, high):
    factor_of = 1.0
    for axis_at, shards_of in shards:
        steps = jax.random.uniform(jax.random.fold_in(jax.random.fold_in(rng, 6), axis_at), (shards_of,), jnp.float32, smallest / len(shards), high / len(shards))
        factor_of = factor_of * jnp.repeat(jnp.exp(steps), dims[axis_at] // shards_of).reshape((-1,) + (1,) * (len(dims) - 1 - axis_at))
    return factor_of


def shared_out(stream_key, own, number, rows, count, top, reach, lean):
    sequence = jax.random.permutation(stream_key, count)
    packed, common = shares(count, rows * top, reach, lean, True), shares(count, rows * top, reach, lean, False)
    places = jnp.arange(count)

    def named(tallies, rotation):
        used = int((tallies > 0).sum())
        fixed = max(1, used // 4)
        moved = fixed + (places - fixed + rotation * (used - fixed)) % max(1, count - fixed)
        return jnp.zeros((count,), jnp.int32).at[sequence[jnp.where(places < fixed, places, moved)]].set(jnp.asarray(tallies, jnp.int32))

    tallies = jnp.where(number % 4 == 0, named(packed, number // 4), named(common, number - number // 4 - 1))
    mixed = jax.random.permutation(jax.random.fold_in(own, 3), count)
    source_of, receiver = mixed[0:count // 2 * 2:2], mixed[1:count // 2 * 2:2]
    margin = jnp.minimum(tallies[source_of] - 1, reach - tallies[receiver]) // 2
    margin = jnp.where((source_of == sequence[0]) | (receiver == sequence[0]) | (tallies[receiver] == 0), 0, jnp.maximum(margin, 0))
    moved = jax.random.randint(jax.random.fold_in(own, 4), (count // 2,), 0, 1 << 20) % (margin + 1)
    tallies = tallies.at[source_of].add(-moved).at[receiver].add(moved)
    members = jnp.searchsorted(jnp.cumsum(tallies), jnp.arange(rows * top), side="right").astype(jnp.int32)
    listing = members.reshape(top, rows).T
    listing = listing[jax.random.permutation(jax.random.fold_in(own, 1), rows)]
    rotation = jax.random.randint(jax.random.fold_in(own, 2), (rows, 1), 0, top)
    return jnp.take_along_axis(listing, (jnp.arange(top)[None, :] + rotation) % top, axis=1)


def shares(count, total, bound, slope, full):
    loads = [(1 << 20) // math.isqrt(standing ** slope) + 1 for standing in range(1, count + 1)]
    largest = bound if full else min(bound, max(-(-total // count), total * loads[0] // sum(loads)))
    least = 1 if total - largest >= count - 1 else 0
    holding, rest = [largest] + [least] * (count - 1), total - largest - least * (count - 1)
    while rest > 0:
        movable = [i for i in range(1, count) if holding[i] < largest] or [i for i in range(1, count) if holding[i] < bound]
        mass, left = sum([loads[i] for i in movable]), rest
        for i in movable:
            more = min(bound - holding[i], max(1, left * loads[i] // mass), rest)
            holding[i] = holding[i] + more
            rest = rest - more
    return np.array(holding)


def noise(own_key, dims, deviation, limit, cuts=(), kind=jnp.bfloat16):
    values = deviation * jax.random.normal(own_key, dims, jnp.float32)
    if cuts:
        values = values * level_of(own_key, dims, cuts, -0.22, 0.18)
    return jnp.clip(values, -limit, limit).astype(kind)


def noise_with(key, extent, scale, reach, split, heavy, kind=jnp.bfloat16):
    result = scale * jax.random.normal(key, extent, jnp.float32)
    if split:
        result = result * level_of(key, extent, split, -0.22, 0.18)
    return jnp.clip(with_spikes(result, jax.random.fold_in(key, 3), *heavy), -reach, reach).astype(kind)


def setup_inputs(seed: int = 0) -> dict:
    streams_of = jax.random.split(jax.random.key(seed), 9)
    currents = noise(streams_of[0], (BRANCHES, EXC), 1.0, 6.0, ((0, 32),), jnp.float32)
    branch_owner_keys = jax.random.split(jax.random.fold_in(streams_of[1], 1), BRANCHES // BR_DEV)
    branch_owner_turns = jax.random.permutation(jax.random.fold_in(streams_of[1], 3), BRANCHES // BR_DEV)
    branch_owner = jax.vmap(lambda own, number: shared_out(jax.random.fold_in(streams_of[1], 2), own, number, BR_DEV, DEVICES, 2, CAP, 2))(branch_owner_keys, branch_owner_turns).reshape((BRANCHES, 2))
    branch_slot = set_ends(jax.random.randint(streams_of[2], (BRANCHES, 2), 0, OWN), jax.random.fold_in(streams_of[2], 1), 0, OWN - 1).astype(jnp.int32)
    history = noise(streams_of[3], (HIST, NODES, EXC), 1.0, 6.0, ((1, 8),))
    coefficients = noise_with(streams_of[4], (SLAB, NODES), NODES ** -0.5, 0.0234375, ((0, 4), (1, 8)), (1, 0, 8, 2.0))
    delays = set_ends(jax.random.randint(streams_of[5], (SLAB // BLK, NODES // BLK), 0, HIST + 1), jax.random.fold_in(streams_of[5], 1), 0, HIST).astype(jnp.int32)
    slab_owner_keys = jax.random.split(jax.random.fold_in(streams_of[6], 1), SLAB_BR // (SLAB_BR // DEVICES))
    slab_owner_turns = jax.random.permutation(jax.random.fold_in(streams_of[6], 3), SLAB_BR // (SLAB_BR // DEVICES))
    slab_owner = jax.vmap(lambda own, number: shared_out(jax.random.fold_in(streams_of[6], 2), own, number, SLAB_BR // DEVICES, DEVICES, 2, SCAP, 1))(slab_owner_keys, slab_owner_turns).reshape((SLAB_BR, 2))
    slab_offset = set_ends(jax.random.randint(streams_of[7], (SLAB_BR, 2), 0, SHARE), jax.random.fold_in(streams_of[7], 1), 0, SHARE - 1).astype(jnp.int32)
    return {"currents": currents, "branch_owner": branch_owner, "branch_slot": branch_slot, "history": history, "coefficients": coefficients, "delays": delays, "slab_owner": slab_owner, "slab_offset": slab_offset}


def reference(currents, branch_owner, branch_slot, history, coefficients, delays, slab_owner, slab_offset):
    ends = branch_owner * OWN + branch_slot
    increment = jnp.zeros((NODES, EXC), jnp.float32)
    increment = increment.at[ends[:, 1]].add(currents)
    increment = increment.at[ends[:, 0]].add(-currents)
    charge_now = (history[0].astype(jnp.float32) + increment).astype(jnp.bfloat16)
    col_blocks = NODES // BLK
    now_blocks = charge_now.reshape(col_blocks, BLK, EXC)
    past_blocks = history.reshape(HIST, col_blocks, BLK, EXC)
    coef_blocks = coefficients.reshape(SLAB // BLK, BLK, NODES)
    column_ids = jnp.arange(col_blocks, dtype=jnp.int32)

    def one_block(pair):
        coef_rows, delay_row = pair
        earlier = past_blocks[jnp.maximum(delay_row - 1, 0), column_ids]
        source = jnp.where((delay_row == 0)[:, None, None], now_blocks, earlier)
        return jnp.dot(coef_rows.astype(jnp.float32), source.reshape(NODES, EXC).astype(jnp.float32), preferred_element_type=jnp.float32)

    potentials = lax.map(one_block, (coef_blocks, delays)).reshape(SLAB, EXC)
    slab_nodes = (slab_owner * SHARE + slab_offset).astype(jnp.int32)
    drops = potentials[slab_nodes[:, 0]] - potentials[slab_nodes[:, 1]]
    return charge_now, drops
```

```python
import functools

import jax
import jax.numpy as jnp
import numpy as np
from jax import lax
from jax.experimental import pallas as pl
from jax.experimental.pallas import tpu as pltpu
from jax.sharding import PartitionSpec as P

F32, BF16, I32 = jnp.float32, jnp.bfloat16, jnp.int32
ALL = ("row", "col")
CHAINS = 4
UNROLL = 2
LANES = 128
FULL = 32767.0
LOW = 107
SIGNS = 9
MEAN = float(1 << 30)


def log2(n):
    bits = int(n).bit_length() - 1
    assert 1 << bits == n
    return bits


def powers():
    lane = lax.broadcasted_iota(I32, (1, LANES), 1)
    up = jnp.full((1, LANES), 2.0**-LOW, F32)
    down = jnp.full((1, LANES), 2.0**LOW, F32)
    for bit in range(log2(LANES)):
        on = lax.bitwise_and(lane, 1 << bit) > 0
        up = jnp.where(on, up * 2.0 ** (1 << bit), up)
        down = jnp.where(on, down * 2.0 ** -(1 << bit), down)
    return up, down


def signed_steps():
    up = np.ldexp(1 / np.float64(FULL), np.arange(LANES) - LOW)
    table = np.zeros(512, np.float32)
    table[1 : LANES + 1] = up
    table[LANES + 1 : 2 * LANES + 1] = -up
    return jnp.asarray(table)


def scale_of(values, up, down):
    most = jnp.max(jnp.abs(values), axis=1, keepdims=True)
    fits = up >= most
    inverse = jnp.max(jnp.where(fits, down, 0.0), axis=1, keepdims=True)
    index = jnp.sum(jnp.where(fits, 0, 1), axis=1, keepdims=True)
    return index, inverse


def coded(values, inverse):
    return jnp.floor(values * (inverse * FULL) + 0.5).astype(I32)


def pair(low, high):
    return lax.bitwise_or(lax.shift_left(high, 16), lax.bitwise_and(low, 0xFFFF))


def low_of(words):
    return lax.shift_right_arithmetic(lax.shift_left(words, 16), 16)


def high_of(words):
    return lax.shift_right_arithmetic(words, 16)


def vmem(n=1):
    return [pl.BlockSpec(memory_space=pltpu.VMEM)] * n


def params(mib, **more):
    return pltpu.CompilerParams(vmem_limit_bytes=mib << 20, **more)


def pack_kernel(current_ref, out_ref):
    values = current_ref[...]
    _, inverse = scale_of(values, *powers())
    codes = coded(values, inverse)
    half = codes.shape[1] // 2
    out_ref[...] = pair(codes[:, :half], codes[:, half:])


def pack(currents):
    rows, scenarios = currents.shape
    return pl.pallas_call(
        pack_kernel,
        out_shape=jax.ShapeDtypeStruct((rows, scenarios // 2), I32),
        in_specs=vmem(1),
        out_specs=vmem()[0],
        compiler_params=params(16),
        name="pack",
    )(currents)


def list_kernel(sizes, current_ref, owner_ref, slot_ref, out_ref, tally_ref):
    rows_of, owned, block, capacity, chain_rows = sizes
    index, _ = scale_of(current_ref[...], *powers())
    count = current_ref.shape[0]
    owner = jnp.concatenate([owner_ref[:, 0:1], owner_ref[:, 1:2]], axis=0)
    slot = jnp.concatenate([slot_ref[:, 0:1], slot_ref[:, 1:2]], axis=0)
    step = jnp.concatenate([index + (LANES + 1), index + 1], axis=0)
    branch = lax.broadcasted_iota(I32, (count, 1), 0)
    branch = jnp.concatenate([branch, branch], axis=0)
    column = lax.shift_right_logical(owner, log2(rows_of))
    node = lax.bitwise_and(owner, rows_of - 1) * owned + slot
    at_block = lax.shift_right_logical(node, log2(block))
    chain = lax.bitwise_and(at_block, CHAINS - 1)
    place = lax.shift_right_logical(at_block, log2(CHAINS)) * block
    place = place + lax.bitwise_and(node, block - 1)
    entry = step + lax.shift_left(place, SIGNS)
    entry = entry + lax.shift_left(branch, SIGNS + log2(chain_rows))
    key = column * CHAINS + chain
    ends = 2 * count
    hit = key == lax.broadcasted_iota(I32, (ends, LANES), 1)
    onehot = jnp.where(hit, 1.0, 0.0).astype(BF16)
    before = lax.broadcasted_iota(I32, (ends, ends), 0) > lax.broadcasted_iota(I32, (ends, ends), 1)
    before = jnp.where(before, 1.0, 0.0).astype(BF16)
    ranks = jnp.dot(before, onehot, preferred_element_type=F32)
    rank = jnp.sum(jnp.where(hit, ranks, 0.0), axis=1, keepdims=True).astype(I32)
    placed = rank == lax.broadcasted_iota(I32, (ends, capacity), 1)
    contract = (((0,), (0,)), ((), ()))
    total = jnp.zeros((LANES, capacity), I32)
    for piece in range(4):
        part = lax.bitwise_and(lax.shift_right_logical(entry, 8 * piece), 255)
        part = jnp.where(placed, part.astype(F32), 0.0).astype(BF16)
        found = lax.dot_general(onehot, part, contract, preferred_element_type=F32)
        total = total + lax.shift_left(found.astype(I32), 8 * piece)
    tally_ref[...] = jnp.sum(jnp.where(hit, 1, 0), axis=0, keepdims=True)
    out_ref[...] = total[: out_ref.shape[0]]


def make_lists(currents, owner, slot, sizes, keys):
    return pl.pallas_call(
        functools.partial(list_kernel, sizes),
        out_shape=(jax.ShapeDtypeStruct((keys, sizes[3]), I32), jax.ShapeDtypeStruct((1, LANES), I32)),
        in_specs=vmem(3),
        out_specs=tuple(vmem(2)),
        compiler_params=params(24),
        name="lists",
    )(currents, owner, slot)


def routes(row_count, col_count):
    col_bits, row_bits = log2(col_count), log2(row_count)
    across = [1 << b for b in (*range(1, col_bits), *([0] if col_bits else []))]
    along = [1 << (b + col_bits) for b in range(1, row_bits)]
    return (across + along, along + across), 1 << col_bits


def masks(steps):
    found = [0]
    for step in steps:
        found = found + [m ^ step for m in found]
    return found


def positions(row_count, col_count):
    orders, core = routes(row_count, col_count)
    devices = row_count * col_count
    table = np.zeros((devices, devices), np.int32)
    for me in range(devices):
        for far, holder in enumerate((me, me ^ core)):
            order = orders[1 if holder & core else 0]
            for at, mask in enumerate(masks(order)):
                table[me, holder ^ mask] = far * (devices // 2) + at
    return table


def gather_steps(row_count, col_count):
    orders, core = routes(row_count, col_count)
    devices = row_count * col_count
    pairs = []
    for first, second in zip(*orders):
        pairs.append([(d, d ^ (second if d & core else first)) for d in range(devices)])
    sibling = [(d, d ^ core) for d in range(devices)]
    return pairs, sibling


def past_kernel(span, block, first, delays_ref, coef_ref, history_ref, start_ref, out_ref, source):
    step = pl.program_id(0)

    @pl.when(step == 0)
    def _():
        out_ref[...] = start_ref[...]

    for i in range(delays_ref.shape[0]):
        for g in range(span):
            delay = delays_ref[i, first + step * span + g]
            at = pl.ds(g * block, block)
            held = history_ref[jnp.maximum(delay - 1, 0), at, :]
            source[i % 2, at, :] = jnp.where(delay > 0, held, jnp.zeros_like(held))
        rows = pl.ds(i * block, block)
        out_ref[rows, :] += jnp.dot(coef_ref[rows, :], source[i % 2], preferred_element_type=F32)


def past_product(delays, coefficients, history, start, block, first, blocks):
    span = 4
    rows = coefficients.shape[0]
    steps, scenarios = history.shape[0], history.shape[2]
    moved = (rows * 2 + steps * scenarios * 2) * block * blocks + 8 * rows * scenarios
    return pl.pallas_call(
        functools.partial(past_kernel, span, block, first),
        out_shape=jax.ShapeDtypeStruct((rows, scenarios), F32),
        grid=(blocks // span,),
        in_specs=[
            pl.BlockSpec(memory_space=pltpu.SMEM),
            pl.BlockSpec((rows, span * block), lambda k: (0, first // span + k)),
            pl.BlockSpec((steps, span * block, scenarios), lambda k: (0, first // span + k, 0)),
            pl.BlockSpec((rows, scenarios), lambda k: (0, 0)),
        ],
        out_specs=pl.BlockSpec((rows, scenarios), lambda k: (0, 0)),
        scratch_shapes=[pltpu.VMEM((2, span * block, scenarios), BF16)],
        compiler_params=params(32),
        cost_estimate=pl.CostEstimate(
            flops=2 * rows * block * blocks * scenarios, bytes_accessed=moved, transcendentals=0
        ),
        name="past",
    )(delays, coefficients, history, start)


def now_kernel(
    sizes,
    lists_ref, base_ref, tally_ref, table_ref, delays_ref, past_ref,
    near_ref, mid_ref, far_ref, last_ref, history_ref, coef_ref,
    charge_ref, out_ref,
    rows, acc, charge, coef, total, todo, row_sem, load_sem, store_sem, coef_sem,
):
    block, capacity, words, slots, chunks = sizes
    devices = base_ref.shape[0]
    row_blocks, col_blocks = delays_ref.shape
    chain_rows = acc.shape[2]
    quarter = rows.shape[0] // 4
    pieces = (near_ref, mid_ref, far_ref, last_ref)
    row_copies = [
        pltpu.make_async_copy(piece, rows.at[pl.ds(n * quarter, quarter)], row_sem.at[n])
        for n, piece in enumerate(pieces)
    ]
    for copy in row_copies:
        copy.start()
    load = pltpu.make_async_copy(history_ref.at[0], charge, load_sem)
    load.start()

    def scan(at, found):
        i = at // col_blocks
        k = at % col_blocks

        @pl.when(delays_ref[i, k] == 0)
        def _():
            todo[found] = at

        return found + jnp.where(delays_ref[i, k] == 0, 1, 0)

    count = lax.fori_loop(0, row_blocks * col_blocks, scan, jnp.int32(0))

    def coef_copy(t):
        at = todo[t]
        i = at // col_blocks
        k = at % col_blocks
        slot = lax.rem(t, slots)
        return pltpu.make_async_copy(
            coef_ref.at[pl.ds(pl.multiple_of(i * block, block), block),
                        pl.ds(pl.multiple_of(k * block, block), block)],
            coef.at[slot],
            coef_sem.at[slot],
        )

    @pl.loop(0, jnp.minimum(count, slots))
    def _(t):
        coef_copy(t).start()

    for chain in range(CHAINS):
        for side in range(2):
            @pl.loop(0, chain_rows // block)
            def _(n):
                at = pl.ds(pl.multiple_of(n * block, block), block)
                acc[chain * 2 + side][at, :] = jnp.zeros((block, LANES), F32)

    for copy in row_copies:
        copy.wait()

    row_shift = SIGNS + log2(chain_rows)

    @pl.loop(0, devices)
    def _(source):
        base = base_ref[source]
        start = source * words
        most = tally_ref[source]

        @pl.loop(0, (most + (UNROLL - 1)) // UNROLL)
        def _(j):
            for u in range(UNROLL):
                for chain in range(CHAINS):
                    entry = lists_ref[start + chain * capacity + j * UNROLL + u]
                    row = base + lax.shift_right_logical(entry, row_shift)
                    place = lax.bitwise_and(lax.shift_right_logical(entry, SIGNS), chain_rows - 1)
                    step = table_ref[lax.bitwise_and(entry, (1 << SIGNS) - 1)]
                    word = rows[pl.ds(row, 1), :]
                    at = pl.ds(place, 1)
                    acc[chain * 2][at, :] += low_of(word).astype(F32) * step
                    acc[chain * 2 + 1][at, :] += high_of(word).astype(F32) * step

    load.wait()

    def store(k):
        at = pl.ds(pl.multiple_of(k * block, block), block)
        return pltpu.make_async_copy(charge.at[at], charge_ref.at[at], store_sem)

    @pl.loop(0, col_blocks // CHAINS)
    def _(group):
        held = pl.ds(pl.multiple_of(group * block, block), block)
        for chain in range(CHAINS):
            k = group * CHAINS + chain
            at = pl.ds(pl.multiple_of(k * block, block), block)
            for side in range(2):
                lanes = slice(side * LANES, (side + 1) * LANES)
                charge[at, lanes] = (charge[at, lanes].astype(F32) + acc[chain * 2 + side][held, :]).astype(BF16)
            store(k).start()

    for i in range(row_blocks):
        total[i] = past_ref[i * block : (i + 1) * block, :]

    @pl.loop(0, count)
    def _(t):
        at = todo[t]
        i = at // col_blocks
        k = at % col_blocks
        slot = lax.rem(t, slots)
        coef_copy(t).wait()
        source = charge[pl.ds(pl.multiple_of(k * block, block), block), :]
        total[i] += jnp.dot(coef[slot], source, preferred_element_type=F32)

        @pl.when(t + slots < count)
        def _():
            coef_copy(t + slots).start()

    turned = jnp.concatenate([total[i].T for i in range(row_blocks)], axis=1)
    up, down = powers()
    nodes = turned.shape[1]
    mean = jnp.sum(turned, axis=1, keepdims=True) * (1.0 / nodes)
    rest = turned - mean
    index, inverse = scale_of(rest, up, down)
    codes = coded(rest, inverse)
    mean_index, mean_inverse = scale_of(mean, up, down)
    mean_code = jnp.floor(mean * mean_inverse * MEAN).astype(I32)
    lane = lax.broadcasted_iota(I32, (turned.shape[0], LANES), 1)
    head = jnp.where(lane == 0, index, jnp.where(lane == 1, mean_index, jnp.where(lane == 2, mean_code, 0)))
    chunk = turned.shape[0] // chunks
    half = chunk // 2
    for c in range(chunks):
        one = slice(c * chunk, c * chunk + half)
        two = slice(c * chunk + half, (c + 1) * chunk)
        out_ref[c, :, :nodes] = pair(codes[one], codes[two])
        out_ref[c, :, nodes : nodes + LANES] = head[one]
        out_ref[c, :, nodes + LANES :] = head[two]

    pltpu.make_async_copy(charge, charge_ref, store_sem).wait()


def now_product(lists, base, tally, table, delays, past, pieces, history, coefficients, block, capacity, words, chunks):
    rows, scenarios = past.shape
    nodes = history.shape[1]
    row_blocks, col_blocks = delays.shape
    slots = 32
    smem = pl.BlockSpec(memory_space=pltpu.SMEM)
    hbm = pl.BlockSpec(memory_space=pl.ANY)
    sizes = (block, capacity, words, slots, chunks)

    def kernel(*refs):
        refs = list(refs)
        at = 14
        acc = refs[at + 1 : at + 1 + 2 * CHAINS]
        now_kernel(sizes, *refs[: at + 1], ListOf(acc), *refs[at + 1 + 2 * CHAINS :])

    return pl.pallas_call(
        kernel,
        out_shape=(
            jax.ShapeDtypeStruct((nodes, scenarios), BF16),
            jax.ShapeDtypeStruct((chunks, scenarios // chunks // 2, rows + 2 * LANES), I32),
        ),
        in_specs=[smem] * 5 + vmem(1) + [hbm] * 6,
        out_specs=(hbm, vmem()[0]),
        scratch_shapes=[
            pltpu.VMEM((4 * pieces[0].shape[0], scenarios // 2), I32),
            *[pltpu.VMEM((nodes // CHAINS, LANES), F32) for _ in range(2 * CHAINS)],
            pltpu.VMEM((nodes, scenarios), BF16),
            pltpu.VMEM((slots, block, block), BF16),
            pltpu.VMEM((row_blocks, block, scenarios), F32),
            pltpu.SMEM((row_blocks * col_blocks,), I32),
            pltpu.SemaphoreType.DMA((4,)),
            pltpu.SemaphoreType.DMA,
            pltpu.SemaphoreType.DMA,
            pltpu.SemaphoreType.DMA((slots,)),
        ],
        compiler_params=params(60),
        cost_estimate=pl.CostEstimate(flops=1 << 30, bytes_accessed=80 << 20, transcendentals=0),
        name="now",
    )(lists, base, tally, table, delays, past, *pieces, history, coefficients)


class ListOf(list):
    @property
    def shape(self):
        return (len(self), 1, self[0].shape[0], self[0].shape[1])


def sum_kernel(got_ref, out_ref):
    sources, half, width = got_ref.shape
    nodes = width - 2 * LANES
    up, _ = powers()
    lane = lax.broadcasted_iota(I32, (half, LANES), 1)

    def power(index):
        return jnp.sum(jnp.where(lane == index, up, 0.0), axis=1, keepdims=True)

    for side in range(2):
        total = jnp.zeros((half, nodes), F32)
        for source in range(sources):
            words = got_ref[source, :, :nodes]
            head = got_ref[source, :, nodes + side * LANES : nodes + (side + 1) * LANES]
            codes = (high_of(words) if side else low_of(words)).astype(F32)
            mean = head[:, 2:3].astype(F32) * (power(head[:, 1:2]) * (1.0 / MEAN))
            total = total + (codes * (power(head[:, 0:1]) * (1.0 / FULL)) + mean)
        out_ref[side * half : (side + 1) * half, :] = total


def sum_columns(got):
    _, half, width = got.shape
    return pl.pallas_call(
        sum_kernel,
        out_shape=jax.ShapeDtypeStruct((2 * half, width - 2 * LANES), F32),
        in_specs=vmem(1),
        out_specs=vmem()[0],
        compiler_params=params(16),
        name="sum",
    )(got)


def drop_kernel(node_ref, potential_ref, out_ref):
    row_count, excitations, nodes = potential_ref.shape
    per_row = nodes // LANES
    groups = excitations // 8

    @pl.loop(0, node_ref.shape[1] // LANES)
    def _(group):
        at = pl.ds(pl.multiple_of(group * LANES, LANES), LANES)
        found = [[None] * groups, [None] * groups]
        for end in range(2):
            node = jnp.broadcast_to(node_ref[pl.ds(end, 1), at], (8, LANES))
            inner = lax.bitwise_and(node, LANES - 1)
            outer = lax.shift_right_logical(node, log2(LANES))
            for e in range(groups):
                value = jnp.zeros((8, LANES), F32)
                for h in range(row_count * per_row):
                    lanes = slice(h % per_row * LANES, (h % per_row + 1) * LANES)
                    held = potential_ref[h // per_row, e * 8 : (e + 1) * 8, lanes]
                    seen = jnp.take_along_axis(held, inner, axis=1, mode="promise_in_bounds")
                    value = jnp.where(outer == h, seen, value)
                found[end][e] = value
        for e in range(groups):
            out_ref[e * 8 : (e + 1) * 8, at] = found[0][e] - found[1][e]


def row_drops(nodes, potentials):
    return pl.pallas_call(
        drop_kernel,
        out_shape=jax.ShapeDtypeStruct((potentials.shape[1], nodes.shape[1]), F32),
        in_specs=vmem(2),
        out_specs=vmem()[0],
        compiler_params=params(24),
        name="drops",
    )(nodes, potentials)


def branch_lists(currents, owner, slot, slab_owner, slab_offset, col_count, share, sizes):
    lists, tally = make_lists(currents, owner, slot, sizes, col_count * CHAINS)
    slab = (slab_owner * share + slab_offset).T.reshape(-1, LANES)
    return lists.reshape(col_count, -1, LANES), tally, slab


def share_lists(lists, tally, slab, row_count, col_count):
    common = jnp.concatenate([tally, slab], axis=0)
    extra = -(lists.shape[1] + common.shape[0]) % 8
    common = jnp.concatenate([common, jnp.zeros((extra, LANES), I32)], axis=0)
    common = jnp.broadcast_to(common[None], (col_count, *common.shape))
    message = jnp.concatenate([lists, common], axis=1)
    message = jnp.broadcast_to(message[None], (row_count, *message.shape)).reshape(-1, LANES)
    return lax.all_to_all(message, ALL, split_axis=0, concat_axis=0, tiled=True)


def local(currents, branch_owner, branch_slot, history, coefficients, delays, slab_owner, slab_offset):
    row_count = lax.axis_size("row")
    col_count = lax.axis_size("col")
    devices = row_count * col_count
    branch_rows, scenarios = currents.shape
    owned = history.shape[1] // row_count
    block = coefficients.shape[1] // delays.shape[1]
    per_owner = 8 * branch_rows // devices
    capacity = -(-min(2 * branch_rows, row_count * per_owner) // LANES) * LANES
    chain_rows = history.shape[1] // CHAINS
    share = coefficients.shape[0] * row_count // devices
    my_row, my_col = lax.axis_index("row"), lax.axis_index("col")
    me = my_row * col_count + my_col
    pairs, sibling = gather_steps(row_count, col_count)
    parts = 4
    col_blocks = delays.shape[1]
    past = jnp.zeros((coefficients.shape[0], scenarios), F32)
    together = lax.optimization_barrier

    def add_past(past, part):
        return past_product(
            delays, coefficients, history, past, block, part * col_blocks // parts, col_blocks // parts
        )

    held = pack(currents)
    jobs = {0: (), 1: (0,), 2: (1,), 3: (2, 3)}
    message = None
    for number, step in enumerate(pairs[:-1]):
        held, past, currents = together((held, past, currents))
        got = lax.ppermute(held, ALL, step)
        for job in jobs.get(number, ()):
            past = add_past(past, job)
        if number == 0:
            lists, tally, slab = branch_lists(
                currents, branch_owner, branch_slot, slab_owner, slab_offset, col_count, share,
                (row_count, owned, block, capacity, chain_rows),
            )
            got, past, lists, tally, slab = together((got, past, lists, tally, slab))
            message = share_lists(lists, tally, slab, row_count, col_count)
        elif number == 2:
            got, past, message = together((got, past, message))
        else:
            got, past = together((got, past))
        held = jnp.concatenate([held, got], axis=0)
    held, past = together((held, past))
    mid = lax.ppermute(held, ALL, pairs[-1])
    far = lax.ppermute(held, ALL, sibling)
    for number in range(len(pairs) - 1, parts):
        for job in jobs[number]:
            past = add_past(past, job)
    mid, past = together((mid, past))
    last = lax.ppermute(mid, ALL, sibling)

    list_tiles = CHAINS * capacity // LANES
    slab_rows = slab_owner.shape[0]
    slab_tiles = 2 * slab_rows // LANES
    width = message.shape[0] // devices
    message = message.reshape(devices, width, LANES)
    tally = lax.dynamic_slice_in_dim(message[:, list_tiles], my_col * CHAINS, CHAINS, 1).max(axis=1)
    row_slab = lax.dynamic_slice_in_dim(message, my_row * col_count, col_count, 0)
    row_slab = row_slab[:, list_tiles + 1 : list_tiles + 1 + slab_tiles]
    row_slab = row_slab.reshape(col_count, 2, slab_rows).transpose(1, 0, 2).reshape(2, col_count * slab_rows)
    table = jnp.asarray(positions(row_count, col_count) * branch_rows)
    base = lax.dynamic_slice_in_dim(table, me, 1, 0)[0]

    charge, partial = now_product(
        message.reshape(-1), base, tally, signed_steps(), delays, past, (held, mid, far, last),
        history, coefficients, block, capacity, width * LANES, col_count,
    )

    got = lax.all_to_all(partial, "col", split_axis=0, concat_axis=0, tiled=True)
    mine = sum_columns(got)
    potentials = lax.all_gather(mine, "row", axis=0, tiled=False)
    found = row_drops(row_slab, potentials)
    excitations = found.shape[0]
    found = found.reshape(excitations, col_count, slab_rows).transpose(1, 0, 2)
    found = lax.all_to_all(found, "col", split_axis=0, concat_axis=0, tiled=True)
    return charge, found.reshape(col_count * excitations, slab_rows).T


def solution(mesh):
    both = P(("row", "col"), None)
    placed = (both, both, both, P(None, "col", None), P("row", "col"), P("row", "col"), both, both)
    return jax.shard_map(
        local,
        mesh=mesh,
        in_specs=placed,
        out_specs=(P("col", None), both),
        check_vma=False,
    )
```

```python
import functools

import jax
import jax.numpy as jnp
import numpy as np
from jax import lax
from jax.experimental import pallas as pl
from jax.experimental.pallas import tpu as pltpu
from jax.sharding import PartitionSpec as P

F32, BF16, I32 = jnp.float32, jnp.bfloat16, jnp.int32
ALL = ("row", "col")
CHAINS = 4
UNROLL = 4
GROUP = 4
LANES = 128
FULL = 32767.0
LOW = 107
PAD = 4
MEAN = float(1 << 30)


def log2(n):
    bits = int(n).bit_length() - 1
    assert 1 << bits == n
    return bits


def powers(shape=(1, LANES), exponent=None):
    if exponent is None:
        exponent = lax.broadcasted_iota(I32, shape, 1 if shape[1] == LANES else 0)
    up = jnp.full(exponent.shape, 2.0**-LOW, F32)
    down = jnp.full(exponent.shape, 2.0**LOW, F32)
    for bit in range(log2(LANES)):
        on = lax.bitwise_and(exponent, 1 << bit) > 0
        up = jnp.where(on, up * 2.0 ** (1 << bit), up)
        down = jnp.where(on, down * 2.0 ** -(1 << bit), down)
    return up, down


def scale_of(values, axis=1):
    up, down = powers((1, LANES) if axis == 1 else (LANES, 1))
    most = jnp.max(jnp.abs(values), axis=axis, keepdims=True)
    fits = up >= most
    inverse = jnp.max(jnp.where(fits, down, 0.0), axis=axis, keepdims=True)
    index = jnp.sum(jnp.where(fits, 0, 1), axis=axis, keepdims=True)
    return index, inverse


def coded(values, inverse):
    return jnp.floor(values * (inverse * FULL) + 0.5).astype(I32)


def pair(low, high):
    return lax.bitwise_or(lax.shift_left(high, 16), lax.bitwise_and(low, 0xFFFF))


def low_of(words):
    return lax.shift_right_arithmetic(lax.shift_left(words, 16), 16)


def high_of(words):
    return lax.shift_right_arithmetic(words, 16)


def vmem(n=1):
    return [pl.BlockSpec(memory_space=pltpu.VMEM)] * n


def params(mib, **more):
    return pltpu.CompilerParams(vmem_limit_bytes=mib << 20, **more)


def pack_kernel(current_ref, out_ref, index_ref):
    values = current_ref[...]
    index, inverse = scale_of(values, axis=0)
    codes = coded(values, inverse)
    half = codes.shape[1] // 2
    out_ref[...] = pair(codes[:, :half], codes[:, half:])
    index_ref[0:1, :] = index[:, :half]
    index_ref[1:2, :] = index[:, half:]


def pack(currents):
    rows, scenarios = currents.shape
    return pl.pallas_call(
        pack_kernel,
        out_shape=(
            jax.ShapeDtypeStruct((rows, scenarios // 2), I32),
            jax.ShapeDtypeStruct((2, scenarios // 2), I32),
        ),
        in_specs=vmem(1),
        out_specs=tuple(vmem(2)),
        compiler_params=params(16),
        name="pack",
    )(currents)


def node_bits(chain_rows):
    return log2(chain_rows) + 2


def list_kernel(sizes, owner_ref, slot_ref, out_ref, tally_ref):
    rows_of, owned, block, capacity, chain_rows = sizes
    count = owner_ref.shape[1]
    ends = 2 * count
    owner = jnp.concatenate([owner_ref[0:1, :], owner_ref[1:2, :]], axis=1)
    slot = jnp.concatenate([slot_ref[0:1, :], slot_ref[1:2, :]], axis=1)
    end = lax.broadcasted_iota(I32, (1, ends), 1)
    branch = lax.bitwise_and(end, count - 1)
    column = lax.shift_right_logical(owner, log2(rows_of))
    node = lax.bitwise_and(owner, rows_of - 1) * owned + slot
    at_block = lax.shift_right_logical(node, log2(block))
    chain = lax.bitwise_and(at_block, CHAINS - 1)
    place = lax.shift_right_logical(at_block, log2(CHAINS)) * block
    place = place + lax.bitwise_and(node, block - 1)
    row = jnp.where(end >= count, 0, count) + branch
    entry = 2 * (place + PAD) + lax.shift_left(2 * row, node_bits(chain_rows))
    key = column * CHAINS + chain
    hit = key == lax.broadcasted_iota(I32, (LANES, ends), 0)
    onehot = jnp.where(hit, 1.0, 0.0).astype(BF16)
    before = lax.broadcasted_iota(I32, (ends, ends), 0) < lax.broadcasted_iota(I32, (ends, ends), 1)
    before = jnp.where(before, 1.0, 0.0).astype(BF16)
    ranks = jnp.dot(onehot, before, preferred_element_type=F32)
    rank = jnp.sum(jnp.where(hit, ranks, 0.0), axis=0, keepdims=True).astype(I32)
    placed = rank == lax.broadcasted_iota(I32, (capacity, ends), 0)
    contract = (((1,), (1,)), ((), ()))
    total = jnp.zeros((LANES, capacity), I32)
    for piece in range(-(-(node_bits(chain_rows) + log2(count) + 2) // 8)):
        part = lax.bitwise_and(lax.shift_right_logical(entry, 8 * piece), 255)
        part = jnp.where(placed, part.astype(F32), 0.0).astype(BF16)
        found = lax.dot_general(onehot, part, contract, preferred_element_type=F32)
        total = total + lax.shift_left(found.astype(I32), 8 * piece)
    ones = jnp.ones((8, ends), BF16)
    tally = lax.dot_general(ones, onehot, contract, preferred_element_type=F32)
    tally_ref[...] = tally[0:1].astype(I32)
    out_ref[...] = total[: out_ref.shape[0]]


def make_lists(owner, slot, sizes, keys):
    return pl.pallas_call(
        functools.partial(list_kernel, sizes),
        out_shape=(jax.ShapeDtypeStruct((keys, sizes[3]), I32), jax.ShapeDtypeStruct((1, LANES), I32)),
        in_specs=vmem(2),
        out_specs=tuple(vmem(2)),
        compiler_params=params(24),
        name="lists",
    )(owner.T, slot.T)


def routes(row_count, col_count):
    col_bits, row_bits = log2(col_count), log2(row_count)
    across = [1 << b for b in (*range(1, col_bits), *([0] if col_bits else []))]
    along = [1 << (b + col_bits) for b in range(1, row_bits)]
    return (across + along, along + across), 1 << col_bits


def masks(steps):
    found = [0]
    for step in steps:
        found = found + [m ^ step for m in found]
    return found


def sources(row_count, col_count):
    orders, core = routes(row_count, col_count)
    devices = row_count * col_count
    table = np.zeros((devices, 2, 2, devices // 4), np.int32)
    for me in range(devices):
        for far, holder in enumerate((me, me ^ core)):
            found = [holder ^ mask for mask in masks(orders[1 if holder & core else 0])]
            table[me, :, far] = np.reshape(found, (2, devices // 4))
    return table.reshape(devices, devices)


def gather_steps(row_count, col_count):
    orders, core = routes(row_count, col_count)
    devices = row_count * col_count
    pairs = []
    for first, second in zip(*orders):
        pairs.append([(d, d ^ (second if d & core else first)) for d in range(devices)])
    sibling = [(d, d ^ core) for d in range(devices)]
    return pairs, sibling


def past_kernel(block, slots, part, parts, todo_ref, owner_ref, start_ref, history_ref, coef_ref, out_ref, coef, source_of, sems):
    count = owner_ref[owner_ref.shape[0] - 1]
    first, last = count * part // parts, count * (part + 1) // parts

    def copies(t):
        slot = lax.rem(t, slots)
        i = owner_ref[t]
        for g in range(GROUP):
            entry = jnp.maximum(todo_ref[t * GROUP + g], 0)
            k = lax.shift_right_logical(entry, 3)
            rows = pl.ds(pl.multiple_of(k * block, block), block)
            yield pltpu.make_async_copy(
                coef_ref.at[pl.ds(pl.multiple_of(i * block, block), block), rows],
                coef.at[slot, :, pl.ds(g * block, block)],
                sems.at[slot, 0, g],
            )
            yield pltpu.make_async_copy(
                history_ref.at[lax.bitwise_and(entry, 7), rows],
                source_of.at[slot, pl.ds(g * block, block)],
                sems.at[slot, 1, g],
            )

    @pl.loop(first, jnp.minimum(first + slots - 1, last))
    def _(t):
        for copy in copies(t):
            copy.start()

    out_ref[...] = start_ref[...]

    @pl.loop(first, last)
    def _(t):
        @pl.when(t + slots - 1 < last)
        def _():
            for copy in copies(t + slots - 1):
                copy.start()

        for copy in copies(t):
            copy.wait()
        slot = lax.rem(t, slots)
        for g in range(1, GROUP):
            @pl.when(todo_ref[t * GROUP + g] < 0)
            def _():
                source_of[slot, g * block : (g + 1) * block, :] = jnp.zeros((block, source_of.shape[2]), BF16)

        out_ref[owner_ref[t]] += jnp.dot(coef[slot], source_of[slot], preferred_element_type=F32)


def past_product(todo, owner, coefficients, history, start, block, part, parts):
    row_blocks, _, scenarios = start.shape
    slots = 6
    moved = (coefficients.size + history.size // history.shape[0] * row_blocks) * 2 // parts
    smem = pl.BlockSpec(memory_space=pltpu.SMEM)
    hbm = pl.BlockSpec(memory_space=pl.ANY)
    return pl.pallas_call(
        functools.partial(past_kernel, block, slots, part, parts),
        out_shape=jax.ShapeDtypeStruct(start.shape, F32),
        in_specs=[smem, smem, *vmem(1), hbm, hbm],
        out_specs=vmem()[0],
        scratch_shapes=[
            pltpu.VMEM((slots, block, GROUP * block), BF16),
            pltpu.VMEM((slots, GROUP * block, scenarios), BF16),
            pltpu.SemaphoreType.DMA((slots, 2, GROUP)),
        ],
        compiler_params=params(32),
        cost_estimate=pl.CostEstimate(
            flops=2 * coefficients.size * scenarios // parts, bytes_accessed=moved, transcendentals=0
        ),
        name="past",
    )(todo, owner, start, history, coefficients)


def scan_kernel(delays_ref, now_ref, now_owner_ref, past_ref, past_owner_ref):
    row_blocks, col_blocks = delays_ref.shape
    found = (jnp.int32(0), jnp.int32(0))
    lists, owners = (now_ref, past_ref), (now_owner_ref, past_owner_ref)
    for i in range(row_blocks):
        first = [at // GROUP for at in found]

        def look(k, at, i=i):
            now, past = at
            for g in range(GROUP):
                delay = delays_ref[i, k * GROUP + g]
                here = jnp.where(delay == 0, 1, 0)
                now_ref[now] = k * GROUP + g
                past_ref[past] = (k * GROUP + g) * 8 + delay - 1
                now, past = now + here, past + (1 - here)
            return now, past

        found = lax.fori_loop(0, col_blocks // GROUP, look, found)
        for g in range(GROUP):
            now_ref[found[0] + g] = -1
            past_ref[found[1] + g] = -1
        found = tuple((at + (GROUP - 1)) // GROUP * GROUP for at in found)
        for n in range(2):
            @pl.loop(first[n], found[n] // GROUP)
            def _(t):
                owners[n][t] = i

    for n in range(2):
        owners[n][owners[n].shape[0] - 1] = found[n] // GROUP


def scan(delays):
    row_blocks, col_blocks = delays.shape
    groups = row_blocks * (col_blocks // GROUP + 1)
    smem = pl.BlockSpec(memory_space=pltpu.SMEM)
    one = (jax.ShapeDtypeStruct((groups * GROUP,), I32), jax.ShapeDtypeStruct((groups + 1,), I32))
    return pl.pallas_call(
        scan_kernel,
        out_shape=one + one,
        in_specs=[smem],
        out_specs=(smem,) * 4,
        name="scan",
    )(delays)


def row_copies(pieces, rows, sems):
    part = pieces[0].shape[0]
    return [
        pltpu.make_async_copy(piece, rows.at[pl.ds(n * part, part)], sems.at[n]) for n, piece in enumerate(pieces)
    ]


def decode(index_ref, order_ref, first, blocks, branch_rows, skip, codes, rows):
    @pl.loop(0, blocks)
    def _(place):
        scales, _ = powers(exponent=index_ref[order_ref[first + place]])
        scales = scales * (1.0 / FULL)
        words = codes[pl.ds(pl.multiple_of((skip + place) * branch_rows, branch_rows), branch_rows), :]
        base = place * (4 * branch_rows)
        for side, part in enumerate((low_of(words), high_of(words))):
            value = part.astype(F32) * scales[side : side + 1, :]
            rows[pl.ds(base + side, branch_rows, stride=2), :] = value
            rows[pl.ds(base + 2 * branch_rows + side, branch_rows, stride=2), :] = -value


def scatter(sizes, first, blocks, lists_ref, order_ref, tally_ref, rows, acc):
    capacity, words, branch_rows = sizes
    bits = node_bits(acc[0].shape[0] // 2 - PAD)

    @pl.loop(0, blocks)
    def _(place):
        source = order_ref[first + place]
        base = place * (4 * branch_rows)
        start = source * words

        @pl.loop(0, (tally_ref[source] + (UNROLL - 1)) // UNROLL)
        def _(j):
            for u in range(UNROLL):
                after = []
                for chain in range(CHAINS):
                    entry = lists_ref[start + chain * capacity + j * UNROLL + u]
                    row = pl.multiple_of(base + lax.shift_right_logical(entry, bits), 2)
                    at = pl.ds(pl.multiple_of(lax.bitwise_and(entry, (1 << bits) - 1), 2), 2)
                    after.append((acc[chain], at, acc[chain][at, :] + rows[pl.ds(row, 2), :]))
                for part, at, value in after:
                    part[at, :] = value


def add_ends(sizes, first, lists_ref, order_ref, tally_ref, index_ref, codes, rows, acc):
    branch_rows = sizes[2]
    blocks = codes.shape[0] // branch_rows
    batch = rows.shape[0] // (4 * branch_rows)
    for skip in range(0, blocks, batch):
        decode(index_ref, order_ref, first + skip, batch, branch_rows, skip, codes, rows)
        scatter(sizes, first + skip, batch, lists_ref, order_ref, tally_ref, rows, acc)


def early_kernel(sizes, lists_ref, order_ref, tally_ref, index_ref, one_ref, two_ref, *more):
    acc, (codes, rows, sems) = more[:CHAINS], more[CHAINS:]
    copies = row_copies((one_ref, two_ref), codes, sems)
    for copy in copies:
        copy.start()
    clear = 512
    for part in acc:
        part[0 : 2 * PAD, :] = jnp.zeros((2 * PAD, LANES), F32)

        @pl.loop(0, part.shape[0] // clear)
        def _(n):
            part[pl.ds(pl.multiple_of(n * clear + 2 * PAD, 8), clear), :] = jnp.zeros((clear, LANES), F32)
    for copy in copies:
        copy.wait()
    add_ends(sizes, 0, lists_ref, order_ref, tally_ref, index_ref, codes, rows, acc)


def early_scatter(lists, order, tally, index, pieces, nodes, sizes):
    smem = pl.BlockSpec(memory_space=pltpu.SMEM)
    hbm = pl.BlockSpec(memory_space=pl.ANY)
    return pl.pallas_call(
        functools.partial(early_kernel, sizes),
        out_shape=tuple(pltpu.VMEM((2 * (nodes // CHAINS + PAD), LANES), F32) for _ in range(CHAINS)),
        in_specs=[smem] * 3 + vmem(1) + [hbm] * 2,
        out_specs=tuple(vmem(CHAINS)),
        scratch_shapes=[
            pltpu.VMEM((2 * pieces[0].shape[0], pieces[0].shape[1]), I32),
            pltpu.VMEM((4 * min(2 * pieces[0].shape[0], 16 * sizes[2]), LANES), F32),
            pltpu.SemaphoreType.DMA((2,)),
        ],
        compiler_params=params(38),
        cost_estimate=pl.CostEstimate(flops=1 << 28, bytes_accessed=32 << 20, transcendentals=0),
        name="early",
    )(lists, order, tally, index, *pieces)


def now_kernel(
    block, slots, chunks, sizes,
    lists_ref, order_ref, tally_ref, todo_ref, owner_ref, past_ref, index_ref,
    one_ref, two_ref, history_ref, coef_ref,
    charge_ref, out_ref, acc,
    codes, rows, charge, coef, source_of, total, row_sem, load_sem, store_sem, coef_sem,
):
    row_blocks, col_blocks = total.shape[0], charge.shape[0] // block
    copies = row_copies((one_ref, two_ref), codes, row_sem)
    for copy in copies:
        copy.start()
    load = pltpu.make_async_copy(history_ref.at[0], charge, load_sem)
    load.start()

    count = owner_ref[owner_ref.shape[0] - 1]

    def coef_copy(t, g):
        i = owner_ref[t]
        k = jnp.maximum(todo_ref[t * GROUP + g], 0)
        slot = lax.rem(t, slots)
        return pltpu.make_async_copy(
            coef_ref.at[pl.ds(pl.multiple_of(i * block, block), block),
                        pl.ds(pl.multiple_of(k * block, block), block)],
            coef.at[slot, :, pl.ds(g * block, block)],
            coef_sem.at[slot, g],
        )

    @pl.loop(0, jnp.minimum(count, slots))
    def _(t):
        for g in range(GROUP):
            coef_copy(t, g).start()

    for copy in copies:
        copy.wait()
    add_ends(sizes, order_ref.shape[0] // 2, lists_ref, order_ref, tally_ref, index_ref, codes, rows, acc)
    load.wait()

    def store(k):
        at = pl.ds(pl.multiple_of(k * block, block), block)
        return pltpu.make_async_copy(charge.at[at], charge_ref.at[at], store_sem)

    @pl.loop(0, col_blocks // CHAINS)
    def _(group):
        for chain in range(CHAINS):
            k = group * CHAINS + chain
            at = pl.ds(pl.multiple_of(k * block, block), block)
            for side in range(2):
                lanes = slice(side * LANES, (side + 1) * LANES)
                held = pl.ds(group * (2 * block) + (2 * PAD + side), block, stride=2)
                charge[at, lanes] = (charge[at, lanes].astype(F32) + acc[chain][held, :]).astype(BF16)
            store(k).start()

    for i in range(row_blocks):
        total[i] = past_ref[i]

    @pl.loop(0, count)
    def _(t):
        for g in range(GROUP):
            k = todo_ref[t * GROUP + g]
            held = charge[pl.ds(pl.multiple_of(jnp.maximum(k, 0) * block, block), block), :]
            source_of[g * block : (g + 1) * block, :] = jnp.where(k >= 0, held, jnp.zeros_like(held))
        for g in range(GROUP):
            coef_copy(t, g).wait()
        slot = lax.rem(t, slots)
        total[owner_ref[t]] += jnp.dot(coef[slot], source_of[...], preferred_element_type=F32)

        @pl.when(t + slots < count)
        def _():
            for g in range(GROUP):
                coef_copy(t + slots, g).start()

    turned = jnp.concatenate([total[i].T for i in range(row_blocks)], axis=1)
    nodes = turned.shape[1]
    mean = jnp.sum(turned, axis=1, keepdims=True) * (1.0 / nodes)
    rest = turned - mean
    index, inverse = scale_of(rest)
    codes = coded(rest, inverse)
    mean_index, mean_inverse = scale_of(mean)
    mean_code = jnp.floor(mean * mean_inverse * MEAN).astype(I32)
    lane = lax.broadcasted_iota(I32, (turned.shape[0], LANES), 1)
    head = jnp.where(lane == 1, mean_index, mean_code)
    head = jnp.where(lane == 0, index, head)
    chunk = turned.shape[0] // chunks
    half = chunk // 2
    for c in range(chunks):
        one = slice(c * chunk, c * chunk + half)
        two = slice(c * chunk + half, (c + 1) * chunk)
        out_ref[c, :, :nodes] = pair(codes[one], codes[two])
        out_ref[c, :, nodes:] = jnp.concatenate([head[one, : LANES // 2], head[two, : LANES // 2]], axis=1)

    pltpu.make_async_copy(charge, charge_ref, store_sem).wait()


def now_product(lists, order, tally, index, todo, owner, past, acc, pieces, history, coefficients, block, chunks, sizes):
    row_blocks, _, scenarios = past.shape
    rows = row_blocks * block
    nodes = history.shape[1]
    slots = 8
    smem = pl.BlockSpec(memory_space=pltpu.SMEM)
    hbm = pl.BlockSpec(memory_space=pl.ANY)
    held = [pltpu.with_memory_space_constraint(part, pltpu.VMEM) for part in acc]
    before, count = 11, len(acc)

    def kernel(*refs):
        sums = refs[before + count + 2 : before + 2 * count + 2]
        ins, outs = refs[:before], refs[before + count : before + count + 2]
        now_kernel(block, slots, chunks, sizes, *ins, *outs, sums, *refs[before + 2 * count + 2 :])

    return pl.pallas_call(
        kernel,
        out_shape=(
            jax.ShapeDtypeStruct((nodes, scenarios), BF16),
            jax.ShapeDtypeStruct((chunks, scenarios // chunks // 2, rows + LANES), I32),
            *[pltpu.VMEM(part.shape, F32) for part in acc],
        ),
        in_specs=[smem] * 5 + vmem(2) + [hbm] * 4 + vmem(count),
        out_specs=(hbm, *vmem(1 + count)),
        input_output_aliases={before + n: 2 + n for n in range(count)},
        scratch_shapes=[
            pltpu.VMEM((2 * pieces[0].shape[0], scenarios // 2), I32),
            pltpu.VMEM((4 * min(2 * pieces[0].shape[0], 16 * sizes[2]), LANES), F32),
            pltpu.VMEM((nodes, scenarios), BF16),
            pltpu.VMEM((slots, block, GROUP * block), BF16),
            pltpu.VMEM((GROUP * block, scenarios), BF16),
            pltpu.VMEM((row_blocks, block, scenarios), F32),
            pltpu.SemaphoreType.DMA((2,)),
            pltpu.SemaphoreType.DMA,
            pltpu.SemaphoreType.DMA,
            pltpu.SemaphoreType.DMA((slots, GROUP)),
        ],
        compiler_params=params(40),
        cost_estimate=pl.CostEstimate(flops=1 << 30, bytes_accessed=80 << 20, transcendentals=0),
        name="now",
    )(lists, order, tally, todo, owner, past, index, *pieces, history, coefficients, *held)[:2]


def sum_kernel(got_ref, out_ref):
    sources, half, width = got_ref.shape
    nodes = width - LANES
    up, _ = powers()
    lane = lax.broadcasted_iota(I32, (half, LANES), 1)

    def power(index):
        return jnp.sum(jnp.where(lane == index, up, 0.0), axis=1, keepdims=True)

    for side in range(2):
        total = jnp.zeros((half, nodes), F32)
        for source in range(sources):
            words = got_ref[source, :, :nodes]
            head = got_ref[source, :, nodes:]
            at = side * (LANES // 2)
            codes = (high_of(words) if side else low_of(words)).astype(F32)
            mean = head[:, at + 2 : at + 3].astype(F32) * (power(head[:, at + 1 : at + 2]) * (1.0 / MEAN))
            total = total + (codes * (power(head[:, at : at + 1]) * (1.0 / FULL)) + mean)
        out_ref[side * half : (side + 1) * half, :] = total


def sum_columns(got):
    _, half, width = got.shape
    return pl.pallas_call(
        sum_kernel,
        out_shape=jax.ShapeDtypeStruct((2 * half, width - LANES), F32),
        in_specs=vmem(1),
        out_specs=vmem()[0],
        compiler_params=params(16),
        name="sum",
    )(got)


def drop_kernel(node_ref, potential_ref, out_ref):
    row_count, excitations, nodes = potential_ref.shape
    per_row = nodes // LANES
    groups = excitations // 8

    @pl.loop(0, node_ref.shape[1] // LANES)
    def _(group):
        at = pl.ds(pl.multiple_of(group * LANES, LANES), LANES)
        found = [[None] * groups, [None] * groups]
        for end in range(2):
            node = jnp.broadcast_to(node_ref[pl.ds(end, 1), at], (8, LANES))
            inner = lax.bitwise_and(node, LANES - 1)
            outer = lax.shift_right_logical(node, log2(LANES))
            for e in range(groups):
                value = jnp.zeros((8, LANES), F32)
                for h in range(row_count * per_row):
                    lanes = slice(h % per_row * LANES, (h % per_row + 1) * LANES)
                    held = potential_ref[h // per_row, e * 8 : (e + 1) * 8, lanes]
                    seen = jnp.take_along_axis(held, inner, axis=1, mode="promise_in_bounds")
                    value = jnp.where(outer == h, seen, value)
                found[end][e] = value
        for e in range(groups):
            out_ref[e * 8 : (e + 1) * 8, at] = found[0][e] - found[1][e]


def row_drops(nodes, potentials):
    return pl.pallas_call(
        drop_kernel,
        out_shape=jax.ShapeDtypeStruct((potentials.shape[1], nodes.shape[1]), F32),
        in_specs=vmem(2),
        out_specs=vmem()[0],
        compiler_params=params(24),
        name="drops",
    )(nodes, potentials)


def branch_lists(index, owner, slot, slab_owner, slab_offset, col_count, share, sizes):
    lists, tally = make_lists(owner, slot, sizes, col_count * CHAINS)
    slab = (slab_owner * share + slab_offset).T.reshape(-1, LANES)
    return lists.reshape(col_count, -1, LANES), tally, jnp.concatenate([index, slab], axis=0)


def share_lists(lists, tally, slab, row_count, col_count):
    common = jnp.concatenate([tally, slab], axis=0)
    extra = -(lists.shape[1] + common.shape[0]) % 8
    common = jnp.concatenate([common, jnp.zeros((extra, LANES), I32)], axis=0)
    common = jnp.broadcast_to(common[None], (col_count, *common.shape))
    message = jnp.concatenate([lists, common], axis=1)
    message = jnp.broadcast_to(message[None], (row_count, *message.shape)).reshape(-1, LANES)
    return lax.all_to_all(message, ALL, split_axis=0, concat_axis=0, tiled=True)


def local(currents, branch_owner, branch_slot, history, coefficients, delays, slab_owner, slab_offset):
    row_count = lax.axis_size("row")
    col_count = lax.axis_size("col")
    devices = row_count * col_count
    branch_rows, scenarios = currents.shape
    owned = history.shape[1] // row_count
    block = coefficients.shape[1] // delays.shape[1]
    per_owner = 8 * branch_rows // devices
    capacity = -(-min(2 * branch_rows, row_count * per_owner) // LANES) * LANES
    chain_rows = history.shape[1] // CHAINS
    share = coefficients.shape[0] * row_count // devices
    my_row, my_col = lax.axis_index("row"), lax.axis_index("col")
    me = my_row * col_count + my_col
    pairs, sibling = gather_steps(row_count, col_count)
    parts = 2
    past = jnp.zeros((delays.shape[0], block, scenarios), F32)
    together = lax.optimization_barrier

    def add_past(past, part):
        return past_product(late, late_owner, coefficients, history, past, block, part, parts)

    held, index = pack(currents)
    order = lax.dynamic_slice_in_dim(jnp.asarray(sources(row_count, col_count)), me, 1, 0)[0]
    jobs = {1: (0,), 2: (1,)}
    message = None
    for number, step in enumerate(pairs[:-1]):
        held, past = together((held, past))
        got = lax.ppermute(held, ALL, step)
        for job in jobs.get(number, ()):
            past = add_past(past, job)
        if number == 0:
            lists, tally, slab = branch_lists(
                index, branch_owner, branch_slot, slab_owner, slab_offset, col_count, share,
                (row_count, owned, block, capacity, chain_rows),
            )
            todo, owner, late, late_owner = scan(delays)
            got, past, lists, tally, slab, late = together((got, past, lists, tally, slab, late))
            message = share_lists(lists, tally, slab, row_count, col_count)
        elif number == len(pairs) - 2:
            got, past, message, order = together((got, past, message, order))
        else:
            got, past = together((got, past))
        held = jnp.concatenate([held, got], axis=0)
    held, past = together((held, past))
    mid = lax.ppermute(held, ALL, pairs[-1])
    far = lax.ppermute(held, ALL, sibling)

    list_tiles = CHAINS * capacity // LANES
    slab_rows = slab_owner.shape[0]
    slab_tiles = 2 * slab_rows // LANES
    width = message.shape[0] // devices
    message = message.reshape(devices, width, LANES)
    tally = lax.dynamic_slice_in_dim(message[:, list_tiles], my_col * CHAINS, CHAINS, 1).max(axis=1)
    row_slab = lax.dynamic_slice_in_dim(message, my_row * col_count, col_count, 0)
    row_slab = row_slab[:, list_tiles + 3 : list_tiles + 3 + slab_tiles]
    index = message[:, list_tiles + 1 : list_tiles + 3]
    row_slab = row_slab.reshape(col_count, 2, slab_rows).transpose(1, 0, 2).reshape(2, col_count * slab_rows)

    lists = message.reshape(-1)
    sizes = (capacity, width * LANES, branch_rows)
    acc = early_scatter(lists, order, tally, index, (held, far), history.shape[1], sizes)
    mid, past, acc = together((mid, past, acc))
    last = lax.ppermute(mid, ALL, sibling)
    charge, partial = now_product(
        lists, order, tally, index, todo, owner, past, acc, (mid, last), history, coefficients,
        block, col_count, sizes,
    )

    got = lax.all_to_all(partial, "col", split_axis=0, concat_axis=0, tiled=True)
    mine = sum_columns(got)
    potentials = lax.all_gather(mine, "row", axis=0, tiled=False)
    found = row_drops(row_slab, potentials)
    excitations = found.shape[0]
    found = found.reshape(excitations, col_count, slab_rows).transpose(1, 0, 2)
    found = lax.all_to_all(found, "col", split_axis=0, concat_axis=0, tiled=True)
    return charge, found.reshape(col_count * excitations, slab_rows).T


def solution(mesh):
    both = P(("row", "col"), None)
    placed = (both, both, both, P(None, "col", None), P("row", "col"), P("row", "col"), both, both)
    return jax.shard_map(
        local,
        mesh=mesh,
        in_specs=placed,
        out_specs=(P("col", None), both),
        check_vma=False,
    )
```

```python
import functools

import jax
import jax.numpy as jnp
import numpy as np
from jax import lax
from jax.experimental import pallas as pl
from jax.experimental.pallas import tpu as pltpu
from jax.sharding import PartitionSpec as P

F32, BF16, I32 = jnp.float32, jnp.bfloat16, jnp.int32
ALL = ("row", "col")
CHAINS = 4
UNROLL = 4
GROUP = 4
LANES = 128
FULL = 32767.0
LOW = 107
PAD = 4
MEAN = float(1 << 30)


def log2(n):
    bits = int(n).bit_length() - 1
    assert 1 << bits == n
    return bits


def powers(shape=(1, LANES), exponent=None):
    if exponent is None:
        exponent = lax.broadcasted_iota(I32, shape, 1 if shape[1] == LANES else 0)
    up = jnp.full(exponent.shape, 2.0**-LOW, F32)
    down = jnp.full(exponent.shape, 2.0**LOW, F32)
    for bit in range(log2(LANES)):
        on = lax.bitwise_and(exponent, 1 << bit) > 0
        up = jnp.where(on, up * 2.0 ** (1 << bit), up)
        down = jnp.where(on, down * 2.0 ** -(1 << bit), down)
    return up, down


def scale_of(values, axis=1):
    up, down = powers((1, LANES) if axis == 1 else (LANES, 1))
    most = jnp.max(jnp.abs(values), axis=axis, keepdims=True)
    fits = up >= most
    inverse = jnp.max(jnp.where(fits, down, 0.0), axis=axis, keepdims=True)
    index = jnp.sum(jnp.where(fits, 0, 1), axis=axis, keepdims=True)
    return index, inverse


def coded(values, inverse):
    return jnp.floor(values * (inverse * FULL) + 0.5).astype(I32)


def pair(low, high):
    return lax.bitwise_or(lax.shift_left(high, 16), lax.bitwise_and(low, 0xFFFF))


def coded_rows(values):
    mean = jnp.sum(values, axis=1, keepdims=True) * (1.0 / values.shape[1])
    rest = values - mean
    index, inverse = scale_of(rest)
    mean_index, mean_inverse = scale_of(mean)
    mean_code = jnp.floor(mean * mean_inverse * MEAN).astype(I32)
    lane = lax.broadcasted_iota(I32, (values.shape[0], LANES), 1)
    head = jnp.where(lane == 0, index, jnp.where(lane == 1, mean_index, mean_code))
    return coded(rest, inverse), head


def both_heads(low, high):
    return jnp.concatenate([low[:, : LANES // 2], high[:, : LANES // 2]], axis=1)


def scale_and_mean(head, side):
    up, _ = powers()
    lane = lax.broadcasted_iota(I32, (head.shape[0], LANES), 1)

    def power(index):
        return jnp.sum(jnp.where(lane == index, up, 0.0), axis=1, keepdims=True)

    at = side * (LANES // 2)
    mean = head[:, at + 2 : at + 3].astype(F32) * (power(head[:, at + 1 : at + 2]) * (1.0 / MEAN))
    return power(head[:, at : at + 1]) * (1.0 / FULL), mean


def low_of(words):
    return lax.shift_right_arithmetic(lax.shift_left(words, 16), 16)


def high_of(words):
    return lax.shift_right_arithmetic(words, 16)


def vmem(n=1):
    return [pl.BlockSpec(memory_space=pltpu.VMEM)] * n


def params(mib, **more):
    return pltpu.CompilerParams(vmem_limit_bytes=mib << 20, **more)


def pack_kernel(current_ref, out_ref, index_ref):
    values = current_ref[...]
    index, inverse = scale_of(values, axis=0)
    codes = coded(values, inverse)
    half = codes.shape[1] // 2
    out_ref[...] = pair(codes[:, :half], codes[:, half:])
    index_ref[0:1, :] = index[:, :half]
    index_ref[1:2, :] = index[:, half:]


def pack(currents):
    rows, scenarios = currents.shape
    return pl.pallas_call(
        pack_kernel,
        out_shape=(
            jax.ShapeDtypeStruct((rows, scenarios // 2), I32),
            jax.ShapeDtypeStruct((2, scenarios // 2), I32),
        ),
        in_specs=vmem(1),
        out_specs=tuple(vmem(2)),
        compiler_params=params(16),
        name="pack",
    )(currents)


def node_bits(chain_rows):
    return log2(chain_rows) + 2


def list_kernel(sizes, owner_ref, slot_ref, out_ref, tally_ref):
    rows_of, owned, block, capacity, chain_rows = sizes
    count = owner_ref.shape[1]
    ends = 2 * count
    owner = jnp.concatenate([owner_ref[0:1, :], owner_ref[1:2, :]], axis=1)
    slot = jnp.concatenate([slot_ref[0:1, :], slot_ref[1:2, :]], axis=1)
    end = lax.broadcasted_iota(I32, (1, ends), 1)
    branch = lax.bitwise_and(end, count - 1)
    column = lax.shift_right_logical(owner, log2(rows_of))
    node = lax.bitwise_and(owner, rows_of - 1) * owned + slot
    at_block = lax.shift_right_logical(node, log2(block))
    chain = lax.bitwise_and(at_block, CHAINS - 1)
    place = lax.shift_right_logical(at_block, log2(CHAINS)) * block
    place = place + lax.bitwise_and(node, block - 1)
    row = jnp.where(end >= count, 0, count) + branch
    entry = 2 * (place + PAD) + lax.shift_left(2 * row, node_bits(chain_rows))
    key = column * CHAINS + chain
    hit = key == lax.broadcasted_iota(I32, (LANES, ends), 0)
    onehot = jnp.where(hit, 1.0, 0.0).astype(BF16)
    before = lax.broadcasted_iota(I32, (ends, ends), 0) < lax.broadcasted_iota(I32, (ends, ends), 1)
    before = jnp.where(before, 1.0, 0.0).astype(BF16)
    ranks = jnp.dot(onehot, before, preferred_element_type=F32)
    rank = jnp.sum(jnp.where(hit, ranks, 0.0), axis=0, keepdims=True).astype(I32)
    placed = rank == lax.broadcasted_iota(I32, (capacity, ends), 0)
    contract = (((1,), (1,)), ((), ()))
    total = jnp.zeros((LANES, capacity), I32)
    for piece in range(-(-(node_bits(chain_rows) + log2(count) + 2) // 8)):
        part = lax.bitwise_and(lax.shift_right_logical(entry, 8 * piece), 255)
        part = jnp.where(placed, part.astype(F32), 0.0).astype(BF16)
        found = lax.dot_general(onehot, part, contract, preferred_element_type=F32)
        total = total + lax.shift_left(found.astype(I32), 8 * piece)
    ones = jnp.ones((8, ends), BF16)
    tally = lax.dot_general(ones, onehot, contract, preferred_element_type=F32)
    tally_ref[...] = tally[0:1].astype(I32)
    out_ref[...] = total[: out_ref.shape[0]]


def make_lists(owner, slot, sizes, keys):
    return pl.pallas_call(
        functools.partial(list_kernel, sizes),
        out_shape=(jax.ShapeDtypeStruct((keys, sizes[3]), I32), jax.ShapeDtypeStruct((1, LANES), I32)),
        in_specs=vmem(2),
        out_specs=tuple(vmem(2)),
        compiler_params=params(24),
        name="lists",
    )(owner.T, slot.T)


def routes(row_count, col_count):
    col_bits, row_bits = log2(col_count), log2(row_count)
    across = [1 << b for b in (*range(1, col_bits), *([0] if col_bits else []))]
    along = [1 << (b + col_bits) for b in range(1, row_bits)]
    return (across + along, along + across), 1 << col_bits


def masks(steps):
    found = [0]
    for step in steps:
        found = found + [m ^ step for m in found]
    return found


def mask_table(row_count, col_count):
    orders, _ = routes(row_count, col_count)
    return jnp.asarray(np.array([masks(order) for order in orders], np.int32))


def source_at(mask_ref, first, place):
    half = mask_ref.shape[1]
    col_count = lax.axis_size("col")
    me = lax.axis_index("row") * col_count + lax.axis_index("col")
    far = place // (half // 2)
    holder = lax.bitwise_xor(me, far * col_count)
    family = lax.bitwise_and(lax.shift_right_logical(holder, log2(col_count)), 1)
    return lax.bitwise_xor(holder, mask_ref[family, first + lax.rem(place, half // 2)])


def gather_steps(row_count, col_count):
    orders, core = routes(row_count, col_count)
    devices = row_count * col_count
    pairs = []
    for first, second in zip(*orders):
        pairs.append([(d, d ^ (second if d & core else first)) for d in range(devices)])
    sibling = [(d, d ^ core) for d in range(devices)]
    return pairs, sibling


def past_kernel(block, slots, region, part, parts, todo_ref, owner_ref, start_ref, history_ref, coef_ref, out_ref, coef, source_of, sems):
    count = owner_ref[owner_ref.shape[0] - 1]
    first, last = count * part // parts, count * (part + 1) // parts

    def copies(t):
        slot = lax.rem(t, slots)
        group = owner_ref[t]
        i = lax.shift_right_logical(group, log2(region))
        for g in range(GROUP):
            entry = jnp.maximum(todo_ref[group + g], 0)
            k = lax.shift_right_logical(entry, 3)
            rows = pl.ds(pl.multiple_of(k * block, block), block)
            yield pltpu.make_async_copy(
                coef_ref.at[pl.ds(pl.multiple_of(i * block, block), block), rows],
                coef.at[slot, :, pl.ds(g * block, block)],
                sems.at[slot, 0, g],
            )
            yield pltpu.make_async_copy(
                history_ref.at[lax.bitwise_and(entry, 7), rows],
                source_of.at[slot, pl.ds(g * block, block)],
                sems.at[slot, 1, g],
            )

    @pl.loop(first, jnp.minimum(first + slots - 1, last))
    def _(t):
        for copy in copies(t):
            copy.start()

    out_ref[...] = start_ref[...]

    @pl.loop(first, last)
    def _(t):
        @pl.when(t + slots - 1 < last)
        def _():
            for copy in copies(t + slots - 1):
                copy.start()

        for copy in copies(t):
            copy.wait()
        slot = lax.rem(t, slots)
        group = owner_ref[t]
        for g in range(1, GROUP):
            @pl.when(todo_ref[group + g] < 0)
            def _():
                source_of[slot, g * block : (g + 1) * block, :] = jnp.zeros((block, source_of.shape[2]), BF16)

        out_ref[lax.shift_right_logical(group, log2(region))] += jnp.dot(coef[slot], source_of[slot], preferred_element_type=F32)


def past_product(todo, owner, coefficients, history, start, block, part, parts):
    row_blocks, _, scenarios = start.shape
    slots = 6
    moved = (coefficients.size + history.size // history.shape[0] * row_blocks) * 2 // parts
    smem = pl.BlockSpec(memory_space=pltpu.SMEM)
    hbm = pl.BlockSpec(memory_space=pl.ANY)
    return pl.pallas_call(
        functools.partial(past_kernel, block, slots, region_of(coefficients.shape[1] // block), part, parts),
        out_shape=jax.ShapeDtypeStruct(start.shape, F32),
        in_specs=[smem, smem, *vmem(1), hbm, hbm],
        out_specs=vmem()[0],
        scratch_shapes=[
            pltpu.VMEM((slots, block, GROUP * block), BF16),
            pltpu.VMEM((slots, GROUP * block, scenarios), BF16),
            pltpu.SemaphoreType.DMA((slots, 2, GROUP)),
        ],
        compiler_params=params(32),
        cost_estimate=pl.CostEstimate(
            flops=2 * coefficients.size * scenarios // parts, bytes_accessed=moved, transcendentals=0
        ),
        name="past",
    )(*(pltpu.with_memory_space_constraint(x, pltpu.HBM) for x in (todo, owner)), start, history, coefficients)


def scan_kernel(region, delays_ref, now_ref, now_group_ref, past_ref, past_group_ref):
    row_blocks, col_blocks = delays_ref.shape

    def look(k, found):
        found = list(found)
        delays = [[delays_ref[i, k * GROUP + g] for i in range(row_blocks)] for g in range(GROUP)]
        for g in range(GROUP):
            for i in range(row_blocks):
                delay = delays[g][i]
                here = jnp.where(delay == 0, 1, 0)
                now_ref[found[2 * i]] = k * GROUP + g
                past_ref[found[2 * i + 1]] = (k * GROUP + g) * 8 + delay - 1
                found[2 * i] += here
                found[2 * i + 1] += 1 - here
        return tuple(found)

    starts = tuple(jnp.int32(region * (n // 2)) for n in range(2 * row_blocks))
    found = lax.fori_loop(0, col_blocks // GROUP, look, starts)
    for n, (blocks, groups) in enumerate(((now_ref, now_group_ref), (past_ref, past_group_ref))):
        total = jnp.int32(0)
        for i in range(row_blocks):
            end = found[2 * i + n]
            for g in range(GROUP):
                blocks[end + g] = -1
            number = (end - region * i + (GROUP - 1)) // GROUP

            @pl.loop(0, number)
            def _(t):
                groups[total + t] = region * i + t * GROUP

            total = total + number
        groups[groups.shape[0] - 1] = total


def region_of(col_blocks):
    return 1 << (col_blocks + GROUP - 1).bit_length()


def scan(delays):
    row_blocks, col_blocks = delays.shape
    region = region_of(col_blocks)
    groups = row_blocks * (col_blocks // GROUP + 1)
    smem = pl.BlockSpec(memory_space=pltpu.SMEM)
    one = (jax.ShapeDtypeStruct((row_blocks * region,), I32), jax.ShapeDtypeStruct((groups + 1,), I32))
    return pl.pallas_call(
        functools.partial(scan_kernel, region),
        out_shape=one + one,
        in_specs=[smem],
        out_specs=(smem,) * 4,
        name="scan",
    )(delays)


def row_copies(pieces, rows, sems):
    part = pieces[0].shape[0]
    return [
        pltpu.make_async_copy(piece, rows.at[pl.ds(n * part, part)], sems.at[n]) for n, piece in enumerate(pieces)
    ]


def decode(head, mask_ref, first, blocks, sizes, skip, codes, rows):
    branch_rows = sizes[2]

    @pl.loop(0, blocks)
    def _(place):
        source = source_at(mask_ref, first, skip + place)
        at = (sizes[0] * CHAINS // LANES) % 8 + 1
        scales, _ = powers(exponent=head[source, at : at + 2, :])
        scales = scales * (1.0 / FULL)
        words = codes[pl.ds(pl.multiple_of((skip + place) * branch_rows, branch_rows), branch_rows), :]
        base = place * (4 * branch_rows)
        for side, part in enumerate((low_of(words), high_of(words))):
            value = part.astype(F32) * scales[side : side + 1, :]
            rows[pl.ds(base + side, branch_rows, stride=2), :] = value
            rows[pl.ds(base + 2 * branch_rows + side, branch_rows, stride=2), :] = -value


def scatter(sizes, first, skip, blocks, lists_ref, mask_ref, rows, acc):
    capacity, words, branch_rows = sizes
    bits = node_bits(acc[0].shape[0] // 2 - PAD)

    @pl.loop(0, blocks)
    def _(place):
        source = source_at(mask_ref, first, skip + place)
        base = place * (4 * branch_rows)
        start = source * words
        tally = start + CHAINS * capacity + lax.axis_index("col") * CHAINS
        most = lists_ref[tally]
        for chain in range(1, CHAINS):
            most = jnp.maximum(most, lists_ref[tally + chain])

        @pl.loop(0, (most + (UNROLL - 1)) // UNROLL)
        def _(j):
            for u in range(UNROLL):
                after = []
                for chain in range(CHAINS):
                    entry = lists_ref[start + chain * capacity + j * UNROLL + u]
                    row = pl.multiple_of(base + lax.shift_right_logical(entry, bits), 2)
                    at = pl.ds(pl.multiple_of(lax.bitwise_and(entry, (1 << bits) - 1), 2), 2)
                    after.append((acc[chain], at, acc[chain][at, :] + rows[pl.ds(row, 2), :]))
                for part, at, value in after:
                    part[at, :] = value


def head_copy(sizes, message_ref, head, sem):
    first = sizes[0] * CHAINS // LANES // 8 * 8
    return pltpu.make_async_copy(message_ref.at[:, pl.ds(first, head.shape[1])], head, sem)


def head_shape(sizes, devices):
    first = sizes[0] * CHAINS // LANES // 8 * 8
    return pltpu.VMEM((devices, sizes[1] // LANES - first, LANES), I32)


def add_ends(sizes, late, lists_ref, mask_ref, head, codes, rows, acc):
    branch_rows = sizes[2]
    first = late * (mask_ref.shape[1] // 2)
    blocks = codes.shape[0] // branch_rows
    batch = rows.shape[0] // (4 * branch_rows)
    for skip in range(0, blocks, batch):
        decode(head, mask_ref, first, batch, sizes, skip, codes, rows)
        scatter(sizes, first, skip, batch, lists_ref, mask_ref, rows, acc)


def early_kernel(sizes, lists_ref, mask_ref, message_ref, one_ref, two_ref, *more):
    acc, (codes, rows, head, sems) = more[:CHAINS], more[CHAINS:]
    copies = [*row_copies((one_ref, two_ref), codes, sems), head_copy(sizes, message_ref, head, sems.at[2])]
    for copy in copies:
        copy.start()
    clear = 512
    for part in acc:
        part[0 : 2 * PAD, :] = jnp.zeros((2 * PAD, LANES), F32)

        @pl.loop(0, part.shape[0] // clear)
        def _(n):
            part[pl.ds(pl.multiple_of(n * clear + 2 * PAD, 8), clear), :] = jnp.zeros((clear, LANES), F32)
    for copy in copies:
        copy.wait()
    add_ends(sizes, 0, lists_ref, mask_ref, head, codes, rows, acc)


def scatter_room(pieces, sizes, devices):
    rows = min(2 * pieces[0].shape[0], 16 * sizes[2])
    return [
        pltpu.VMEM((2 * pieces[0].shape[0], LANES), I32),
        pltpu.VMEM((4 * rows, LANES), F32),
        head_shape(sizes, devices),
    ], (2 * pieces[0].shape[0] + 4 * rows + devices * 16) * LANES * 4 >> 20


def early_scatter(message, mask, pieces, nodes, sizes):
    room, mib = scatter_room(pieces, sizes, message.shape[0])
    smem = pl.BlockSpec(memory_space=pltpu.SMEM)
    hbm = pl.BlockSpec(memory_space=pl.ANY)
    return pl.pallas_call(
        functools.partial(early_kernel, sizes),
        out_shape=tuple(pltpu.VMEM((2 * (nodes // CHAINS + PAD), LANES), F32) for _ in range(CHAINS)),
        in_specs=[smem] * 2 + [hbm] * 3,
        out_specs=tuple(vmem(CHAINS)),
        scratch_shapes=[*room, pltpu.SemaphoreType.DMA((3,))],
        compiler_params=params(mib + 4),
        cost_estimate=pl.CostEstimate(flops=1 << 28, bytes_accessed=32 << 20, transcendentals=0),
        name="early",
    )(message.reshape(-1), mask, message, *pieces)


def now_kernel(
    block, slots, chunks, sizes,
    lists_ref, mask_ref, todo_ref, owner_ref, past_ref, message_ref,
    one_ref, two_ref, history_ref, coef_ref,
    charge_ref, out_ref, acc,
    codes, rows, head, charge, coef, source_of, total, row_sem, load_sem, store_sem, coef_sem,
):
    row_blocks, col_blocks = total.shape[0], charge.shape[0] // block
    copies = [*row_copies((one_ref, two_ref), codes, row_sem), head_copy(sizes, message_ref, head, row_sem.at[2])]
    for copy in copies:
        copy.start()
    load = pltpu.make_async_copy(history_ref.at[0], charge, load_sem)
    load.start()

    count = owner_ref[owner_ref.shape[0] - 1]
    region_bits = log2(region_of(col_blocks))

    def coef_copy(t, g):
        i = lax.shift_right_logical(owner_ref[t], region_bits)
        k = jnp.maximum(todo_ref[owner_ref[t] + g], 0)
        slot = lax.rem(t, slots)
        return pltpu.make_async_copy(
            coef_ref.at[pl.ds(pl.multiple_of(i * block, block), block),
                        pl.ds(pl.multiple_of(k * block, block), block)],
            coef.at[slot, :, pl.ds(g * block, block)],
            coef_sem.at[slot, g],
        )

    @pl.loop(0, jnp.minimum(count, slots))
    def _(t):
        for g in range(GROUP):
            coef_copy(t, g).start()

    for copy in copies:
        copy.wait()
    add_ends(sizes, 1, lists_ref, mask_ref, head, codes, rows, acc)
    load.wait()

    def store(k):
        at = pl.ds(pl.multiple_of(k * block, block), block)
        return pltpu.make_async_copy(charge.at[at], charge_ref.at[at], store_sem)

    @pl.loop(0, col_blocks // CHAINS)
    def _(group):
        for chain in range(CHAINS):
            k = group * CHAINS + chain
            at = pl.ds(pl.multiple_of(k * block, block), block)
            for side in range(2):
                lanes = slice(side * LANES, (side + 1) * LANES)
                held = pl.ds(group * (2 * block) + (2 * PAD + side), block, stride=2)
                charge[at, lanes] = (charge[at, lanes].astype(F32) + acc[chain][held, :]).astype(BF16)
            store(k).start()

    for i in range(row_blocks):
        total[i] = past_ref[i]

    @pl.loop(0, count)
    def _(t):
        for g in range(GROUP):
            k = todo_ref[owner_ref[t] + g]
            held = charge[pl.ds(pl.multiple_of(jnp.maximum(k, 0) * block, block), block), :]
            source_of[g * block : (g + 1) * block, :] = jnp.where(k >= 0, held, jnp.zeros_like(held))
        for g in range(GROUP):
            coef_copy(t, g).wait()
        slot = lax.rem(t, slots)
        total[lax.shift_right_logical(owner_ref[t], region_bits)] += jnp.dot(coef[slot], source_of[...], preferred_element_type=F32)

        @pl.when(t + slots < count)
        def _():
            for g in range(GROUP):
                coef_copy(t + slots, g).start()

    turned = jnp.concatenate([total[i].T for i in range(row_blocks)], axis=1)
    nodes = turned.shape[1]
    codes, head = coded_rows(turned)
    chunk = turned.shape[0] // chunks
    half = chunk // 2
    for c in range(chunks):
        one = slice(c * chunk, c * chunk + half)
        two = slice(c * chunk + half, (c + 1) * chunk)
        out_ref[c, :, :nodes] = pair(codes[one], codes[two])
        out_ref[c, :, nodes:] = both_heads(head[one], head[two])

    pltpu.make_async_copy(charge, charge_ref, store_sem).wait()


def now_product(message, mask, todo, owner, past, acc, pieces, history, coefficients, block, chunks, sizes):
    row_blocks, _, scenarios = past.shape
    rows = row_blocks * block
    nodes = history.shape[1]
    slots = 8
    smem = pl.BlockSpec(memory_space=pltpu.SMEM)
    hbm = pl.BlockSpec(memory_space=pl.ANY)
    held = [pltpu.with_memory_space_constraint(part, pltpu.VMEM) for part in acc]
    before, count = 10, len(acc)
    room, mib = scatter_room(pieces, sizes, message.shape[0])
    mib += (nodes * 2 + rows * 4 * 6) * scenarios + slots * GROUP * block * block * 2 >> 20

    def kernel(*refs):
        sums = refs[before + count + 2 : before + 2 * count + 2]
        ins, outs = refs[:before], refs[before + count : before + count + 2]
        now_kernel(block, slots, chunks, sizes, *ins, *outs, sums, *refs[before + 2 * count + 2 :])

    return pl.pallas_call(
        kernel,
        out_shape=(
            jax.ShapeDtypeStruct((nodes, scenarios), BF16),
            jax.ShapeDtypeStruct((chunks, scenarios // chunks // 2, rows + LANES), I32),
            *[pltpu.VMEM(part.shape, F32) for part in acc],
        ),
        in_specs=[smem] * 4 + vmem(1) + [hbm] * 5 + vmem(count),
        out_specs=(hbm, *vmem(1 + count)),
        input_output_aliases={before + n: 2 + n for n in range(count)},
        scratch_shapes=[
            *room,
            pltpu.VMEM((nodes, scenarios), BF16),
            pltpu.VMEM((slots, block, GROUP * block), BF16),
            pltpu.VMEM((GROUP * block, scenarios), BF16),
            pltpu.VMEM((row_blocks, block, scenarios), F32),
            pltpu.SemaphoreType.DMA((3,)),
            pltpu.SemaphoreType.DMA,
            pltpu.SemaphoreType.DMA,
            pltpu.SemaphoreType.DMA((slots, GROUP)),
        ],
        compiler_params=params(mib + 6),
        cost_estimate=pl.CostEstimate(flops=1 << 30, bytes_accessed=80 << 20, transcendentals=0),
        name="now",
    )(message.reshape(-1), mask, todo, owner, past, message, *pieces, history, coefficients, *held)[:2]


def sum_kernel(got_ref, out_ref):
    sources, half, width = got_ref.shape
    nodes = width - LANES
    codes, heads = [], []
    for side in range(2):
        total = jnp.zeros((half, nodes), F32)
        for source in range(sources):
            words = got_ref[source, :, :nodes]
            scale, mean = scale_and_mean(got_ref[source, :, nodes:], side)
            total = total + ((high_of(words) if side else low_of(words)).astype(F32) * scale + mean)
        code, head = coded_rows(total)
        codes.append(code)
        heads.append(head)
    out_ref[:, :nodes] = pair(*codes)
    out_ref[:, nodes:] = both_heads(*heads)


def sum_columns(got):
    return pl.pallas_call(
        sum_kernel,
        out_shape=jax.ShapeDtypeStruct(got.shape[1:], I32),
        in_specs=vmem(1),
        out_specs=vmem()[0],
        compiler_params=params(16),
        name="sum",
    )(got)


def drop_kernel(node_ref, word_ref, out_ref):
    row_count, half, width = word_ref.shape
    nodes = width - LANES
    per_row = nodes // LANES
    worth = [[scale_and_mean(word_ref[r, :, nodes:], side) for side in range(2)] for r in range(row_count)]

    @pl.loop(0, node_ref.shape[1] // LANES)
    def _(group):
        at = pl.ds(pl.multiple_of(group * LANES, LANES), LANES)
        found = []
        for end in range(2):
            node = jnp.broadcast_to(node_ref[pl.ds(end, 1), at], (8, LANES))
            inner = lax.bitwise_and(node, LANES - 1)
            outer = lax.shift_right_logical(node, log2(LANES))
            row = lax.shift_right_logical(node, log2(nodes))
            for e in range(0, half, 8):
                values = [jnp.zeros((8, LANES), F32)] * 2
                for r in range(row_count):
                    word = jnp.zeros((8, LANES), I32)
                    for h in range(per_row):
                        held = word_ref[r, e : e + 8, h * LANES : (h + 1) * LANES]
                        seen = jnp.take_along_axis(held, inner, axis=1, mode="promise_in_bounds")
                        word = jnp.where(outer == r * per_row + h, seen, word)
                    for side, code in enumerate((low_of(word), high_of(word))):
                        scale, mean = worth[r][side]
                        value = code.astype(F32) * scale[e : e + 8] + mean[e : e + 8]
                        values[side] = jnp.where(row == r, value, values[side])
                found.append(values)
        groups = len(found) // 2
        for e in range(groups):
            for side in range(2):
                rows = pl.ds(side * half + e * 8, 8)
                out_ref[rows, at] = found[e][side] - found[groups + e][side]


def row_drops(nodes, words):
    return pl.pallas_call(
        drop_kernel,
        out_shape=jax.ShapeDtypeStruct((2 * words.shape[1], nodes.shape[1]), F32),
        in_specs=vmem(2),
        out_specs=vmem()[0],
        compiler_params=params(24),
        name="drops",
    )(nodes, words)


def branch_lists(index, owner, slot, slab_owner, slab_offset, col_count, share, sizes):
    lists, tally = make_lists(owner, slot, sizes, col_count * CHAINS)
    slab = (slab_owner * share + slab_offset).T.reshape(-1, LANES)
    return lists.reshape(col_count, -1, LANES), tally, jnp.concatenate([index, slab], axis=0)


def share_lists(lists, tally, slab, row_count, col_count):
    common = jnp.concatenate([tally, slab], axis=0)
    extra = -(lists.shape[1] + common.shape[0]) % 8
    common = jnp.concatenate([common, jnp.zeros((extra, LANES), I32)], axis=0)
    common = jnp.broadcast_to(common[None], (col_count, *common.shape))
    message = jnp.concatenate([lists, common], axis=1)
    message = jnp.broadcast_to(message[None], (row_count, *message.shape)).reshape(-1, LANES)
    return lax.all_to_all(message, ALL, split_axis=0, concat_axis=0, tiled=True)


def local(currents, branch_owner, branch_slot, history, coefficients, delays, slab_owner, slab_offset):
    row_count = lax.axis_size("row")
    col_count = lax.axis_size("col")
    devices = row_count * col_count
    branch_rows, scenarios = currents.shape
    owned = history.shape[1] // row_count
    block = coefficients.shape[1] // delays.shape[1]
    per_owner = 8 * branch_rows // devices
    capacity = -(-min(2 * branch_rows, row_count * per_owner) // LANES) * LANES
    chain_rows = history.shape[1] // CHAINS
    share = coefficients.shape[0] * row_count // devices
    my_row, my_col = lax.axis_index("row"), lax.axis_index("col")
    me = my_row * col_count + my_col
    pairs, sibling = gather_steps(row_count, col_count)
    parts = 2
    past = jnp.zeros((delays.shape[0], block, scenarios), F32)
    together = lax.optimization_barrier

    def add_past(past, part):
        return past_product(late, late_owner, coefficients, history, past, block, part, parts)

    held, index = pack(currents)
    jobs = {1: (0,), 2: (1,)}
    message = None
    for number, step in enumerate(pairs[:-1]):
        held, past = together((held, past))
        got = lax.ppermute(held, ALL, step)
        for job in jobs.get(number, ()):
            past = add_past(past, job)
        if number == 0:
            lists, tally, slab = branch_lists(
                index, branch_owner, branch_slot, slab_owner, slab_offset, col_count, share,
                (row_count, owned, block, capacity, chain_rows),
            )
            todo, owner, late, late_owner = scan(delays)
            got, past, lists, tally, slab, late = together((got, past, lists, tally, slab, late))
            message = share_lists(lists, tally, slab, row_count, col_count)
        elif number == len(pairs) - 2:
            got, past, message = together((got, past, message))
        else:
            got, past = together((got, past))
        held = jnp.concatenate([held, got], axis=0)
    held, past = together((held, past))
    mid = lax.ppermute(held, ALL, pairs[-1])
    far = lax.ppermute(held, ALL, sibling)

    list_tiles = CHAINS * capacity // LANES
    slab_rows = slab_owner.shape[0]
    slab_tiles = 2 * slab_rows // LANES
    width = message.shape[0] // devices
    message = message.reshape(devices, width, LANES)
    row_slab = lax.dynamic_slice_in_dim(message, my_row * col_count, col_count, 0)
    row_slab = row_slab[:, list_tiles + 3 : list_tiles + 3 + slab_tiles]
    row_slab = row_slab.reshape(col_count, 2, slab_rows).transpose(1, 0, 2).reshape(2, col_count * slab_rows)

    mask = mask_table(row_count, col_count)
    sizes = (capacity, width * LANES, branch_rows)
    acc = early_scatter(message, mask, (held, far), history.shape[1], sizes)
    mid, past, acc = together((mid, past, acc))
    last = lax.ppermute(mid, ALL, sibling)
    charge, partial = now_product(
        message, mask, todo, owner, past, acc, (mid, last), history, coefficients,
        block, col_count, sizes,
    )

    got = lax.all_to_all(partial, "col", split_axis=0, concat_axis=0, tiled=True)
    mine = sum_columns(got)
    potentials = lax.all_gather(mine, "row", axis=0, tiled=False)
    found = row_drops(row_slab, potentials)
    excitations = found.shape[0]
    found = found.reshape(excitations, col_count, slab_rows).transpose(1, 0, 2)
    found = lax.all_to_all(found, "col", split_axis=0, concat_axis=0, tiled=True)
    return charge, found.reshape(col_count * excitations, slab_rows).T


def solution(mesh):
    both = P(("row", "col"), None)
    placed = (both, both, both, P(None, "col", None), P("row", "col"), P("row", "col"), both, both)
    return jax.shard_map(
        local,
        mesh=mesh,
        in_specs=placed,
        out_specs=(P("col", None), both),
        check_vma=False,
    )
```

```python
import functools

import jax
import jax.numpy as jnp
import numpy as np
from jax import lax
from jax.experimental import pallas as pl
from jax.experimental.pallas import tpu as pltpu
from jax.sharding import PartitionSpec as P

F32, BF16, I32 = jnp.float32, jnp.bfloat16, jnp.int32
ALL = ("row", "col")
CHAINS = 4
UNROLL = 8
GROUP = 4
LANES = 128
FULL = 32767.0
LOW = 107
PAD = 4
MEAN = float(1 << 30)


def log2(n):
    bits = int(n).bit_length() - 1
    assert 1 << bits == n
    return bits


def powers(shape=(1, LANES), exponent=None):
    if exponent is None:
        exponent = lax.broadcasted_iota(I32, shape, 1 if shape[1] == LANES else 0)
    up = jnp.full(exponent.shape, 2.0**-LOW, F32)
    down = jnp.full(exponent.shape, 2.0**LOW, F32)
    for bit in range(log2(LANES)):
        on = lax.bitwise_and(exponent, 1 << bit) > 0
        up = jnp.where(on, up * 2.0 ** (1 << bit), up)
        down = jnp.where(on, down * 2.0 ** -(1 << bit), down)
    return up, down


def scale_of(values, axis=1):
    up, down = powers((1, LANES) if axis == 1 else (LANES, 1))
    most = jnp.max(jnp.abs(values), axis=axis, keepdims=True)
    fits = up >= most
    inverse = jnp.max(jnp.where(fits, down, 0.0), axis=axis, keepdims=True)
    index = jnp.sum(jnp.where(fits, 0, 1), axis=axis, keepdims=True)
    return index, inverse


def coded(values, inverse):
    return jnp.floor(values * (inverse * FULL) + 0.5).astype(I32)


def pair(low, high):
    return lax.bitwise_or(lax.shift_left(high, 16), lax.bitwise_and(low, 0xFFFF))


def coded_rows(values):
    mean = jnp.sum(values, axis=1, keepdims=True) * (1.0 / values.shape[1])
    rest = values - mean
    index, inverse = scale_of(rest)
    mean_index, mean_inverse = scale_of(mean)
    mean_code = jnp.floor(mean * mean_inverse * MEAN).astype(I32)
    lane = lax.broadcasted_iota(I32, (values.shape[0], LANES), 1)
    head = jnp.where(lane == 0, index, jnp.where(lane == 1, mean_index, mean_code))
    return coded(rest, inverse), head


def both_heads(low, high):
    return jnp.concatenate([low[:, : LANES // 2], high[:, : LANES // 2]], axis=1)


def scale_and_mean(head, side):
    up, _ = powers()
    lane = lax.broadcasted_iota(I32, (head.shape[0], LANES), 1)

    def power(index):
        return jnp.sum(jnp.where(lane == index, up, 0.0), axis=1, keepdims=True)

    at = side * (LANES // 2)
    mean = head[:, at + 2 : at + 3].astype(F32) * (power(head[:, at + 1 : at + 2]) * (1.0 / MEAN))
    return power(head[:, at : at + 1]) * (1.0 / FULL), mean


def low_of(words):
    return lax.shift_right_arithmetic(lax.shift_left(words, 16), 16)


def high_of(words):
    return lax.shift_right_arithmetic(words, 16)


def vmem(n=1):
    return [pl.BlockSpec(memory_space=pltpu.VMEM)] * n


def params(mib, **more):
    return pltpu.CompilerParams(vmem_limit_bytes=mib << 20, **more)


def pack_kernel(current_ref, out_ref, index_ref):
    values = current_ref[...]
    index, inverse = scale_of(values, axis=0)
    codes = coded(values, inverse)
    half = codes.shape[1] // 2
    out_ref[...] = pair(codes[:, :half], codes[:, half:])
    index_ref[0:1, :] = index[:, :half]
    index_ref[1:2, :] = index[:, half:]


def pack(currents):
    rows, scenarios = currents.shape
    return pl.pallas_call(
        pack_kernel,
        out_shape=(
            jax.ShapeDtypeStruct((rows, scenarios // 2), I32),
            jax.ShapeDtypeStruct((2, scenarios // 2), I32),
        ),
        in_specs=vmem(1),
        out_specs=tuple(vmem(2)),
        compiler_params=params(16),
        name="pack",
    )(currents)


def node_bits(chain_rows):
    return log2(chain_rows) + 2


def list_kernel(sizes, share, owner_ref, slot_ref, slab_owner_ref, slab_offset_ref, out_ref, tally_ref, slab_ref):
    rows_of, owned, block, capacity, chain_rows = sizes
    slab_ref[...] = slab_owner_ref[...] * share + slab_offset_ref[...]
    count = owner_ref.shape[1]
    ends = 2 * count
    owner = jnp.concatenate([owner_ref[0:1, :], owner_ref[1:2, :]], axis=1)
    slot = jnp.concatenate([slot_ref[0:1, :], slot_ref[1:2, :]], axis=1)
    end = lax.broadcasted_iota(I32, (1, ends), 1)
    branch = lax.bitwise_and(end, count - 1)
    column = lax.shift_right_logical(owner, log2(rows_of))
    node = lax.bitwise_and(owner, rows_of - 1) * owned + slot
    at_block = lax.shift_right_logical(node, log2(block))
    chain = lax.bitwise_and(at_block, CHAINS - 1)
    place = lax.shift_right_logical(at_block, log2(CHAINS)) * block
    place = place + lax.bitwise_and(node, block - 1)
    row = jnp.where(end >= count, 0, count) + branch
    entry = 2 * (place + PAD) + lax.shift_left(2 * row, node_bits(chain_rows))
    key = column * CHAINS + chain
    hit = key == lax.broadcasted_iota(I32, (LANES, ends), 0)
    onehot = jnp.where(hit, 1.0, 0.0).astype(BF16)
    before = lax.broadcasted_iota(I32, (ends, ends), 0) < lax.broadcasted_iota(I32, (ends, ends), 1)
    before = jnp.where(before, 1.0, 0.0).astype(BF16)
    ranks = jnp.dot(onehot, before, preferred_element_type=F32)
    rank = jnp.sum(jnp.where(hit, ranks, 0.0), axis=0, keepdims=True).astype(I32)
    placed = rank == lax.broadcasted_iota(I32, (capacity, ends), 0)
    contract = (((1,), (1,)), ((), ()))
    total = jnp.zeros((LANES, capacity), I32)
    for piece in range(-(-(node_bits(chain_rows) + log2(count) + 2) // 8)):
        part = lax.bitwise_and(lax.shift_right_logical(entry, 8 * piece), 255)
        part = jnp.where(placed, part.astype(F32), 0.0).astype(BF16)
        found = lax.dot_general(onehot, part, contract, preferred_element_type=F32)
        total = total + lax.shift_left(found.astype(I32), 8 * piece)
    ones = jnp.ones((8, ends), BF16)
    tally = lax.dot_general(ones, onehot, contract, preferred_element_type=F32)
    tally_ref[...] = tally[0:1].astype(I32)
    out_ref[...] = total[: out_ref.shape[0]]


def make_lists(owner, slot, slab_owner, slab_offset, share, sizes, keys):
    arrays = [pltpu.with_memory_space_constraint(x.T, pltpu.HBM) for x in (owner, slot, slab_owner, slab_offset)]
    return pl.pallas_call(
        functools.partial(list_kernel, sizes, share),
        out_shape=(
            jax.ShapeDtypeStruct((keys, sizes[3]), I32),
            jax.ShapeDtypeStruct((1, LANES), I32),
            jax.ShapeDtypeStruct(arrays[2].shape, I32),
        ),
        in_specs=vmem(4),
        out_specs=tuple(vmem(3)),
        compiler_params=params(24),
        name="lists",
    )(*arrays)


def routes(row_count, col_count):
    col_bits, row_bits = log2(col_count), log2(row_count)
    across = [1 << b for b in (*range(1, col_bits), *([0] if col_bits else []))]
    along = [1 << (b + col_bits) for b in range(1, row_bits)]
    return (across + along, along + across), 1 << col_bits


def masks(steps):
    found = [0]
    for step in steps:
        found = found + [m ^ step for m in found]
    return found


def mask_table(row_count, col_count):
    orders, _ = routes(row_count, col_count)
    return jnp.asarray(np.array([masks(order) for order in orders], np.int32))


def source_at(mask_ref, first, place):
    half = mask_ref.shape[1]
    col_count = lax.axis_size("col")
    me = lax.axis_index("row") * col_count + lax.axis_index("col")
    far = place // (half // 2)
    holder = lax.bitwise_xor(me, far * col_count)
    family = lax.bitwise_and(lax.shift_right_logical(holder, log2(col_count)), 1)
    return lax.bitwise_xor(holder, mask_ref[family, first + lax.rem(place, half // 2)])


def gather_steps(row_count, col_count):
    orders, core = routes(row_count, col_count)
    devices = row_count * col_count
    pairs = []
    for first, second in zip(*orders):
        pairs.append([(d, d ^ (second if d & core else first)) for d in range(devices)])
    sibling = [(d, d ^ core) for d in range(devices)]
    return pairs, sibling


def past_kernel(block, slots, region, part, parts, todo_ref, owner_ref, start_ref, history_ref, coef_ref, out_ref, coef, source_of, sems):
    count = owner_ref[owner_ref.shape[0] - 1]
    first, last = count * part // parts, count * (part + 1) // parts

    def copies(t):
        slot = lax.rem(t, slots)
        group = owner_ref[t]
        i = lax.shift_right_logical(group, log2(region))
        for g in range(GROUP):
            entry = jnp.maximum(todo_ref[group + g], 0)
            k = lax.shift_right_logical(entry, 3)
            rows = pl.ds(pl.multiple_of(k * block, block), block)
            yield pltpu.make_async_copy(
                coef_ref.at[pl.ds(pl.multiple_of(i * block, block), block), rows],
                coef.at[slot, :, pl.ds(g * block, block)],
                sems.at[slot, 0, g],
            )
            yield pltpu.make_async_copy(
                history_ref.at[lax.bitwise_and(entry, 7), rows],
                source_of.at[slot, pl.ds(g * block, block)],
                sems.at[slot, 1, g],
            )

    @pl.loop(first, jnp.minimum(first + slots - 1, last))
    def _(t):
        for copy in copies(t):
            copy.start()

    out_ref[...] = start_ref[...]

    @pl.loop(first, last)
    def _(t):
        @pl.when(t + slots - 1 < last)
        def _():
            for copy in copies(t + slots - 1):
                copy.start()

        for copy in copies(t):
            copy.wait()
        slot = lax.rem(t, slots)
        group = owner_ref[t]
        for g in range(1, GROUP):
            @pl.when(todo_ref[group + g] < 0)
            def _():
                source_of[slot, g * block : (g + 1) * block, :] = jnp.zeros((block, source_of.shape[2]), BF16)

        out_ref[lax.shift_right_logical(group, log2(region))] += jnp.dot(coef[slot], source_of[slot], preferred_element_type=F32)


def past_product(todo, owner, coefficients, history, start, block, part, parts):
    row_blocks, _, scenarios = start.shape
    slots = 6
    moved = (coefficients.size + history.size // history.shape[0] * row_blocks) * 2 // parts
    smem = pl.BlockSpec(memory_space=pltpu.SMEM)
    hbm = pl.BlockSpec(memory_space=pl.ANY)
    return pl.pallas_call(
        functools.partial(past_kernel, block, slots, region_of(coefficients.shape[1] // block), part, parts),
        out_shape=jax.ShapeDtypeStruct(start.shape, F32),
        in_specs=[smem, smem, *vmem(1), hbm, hbm],
        out_specs=vmem()[0],
        scratch_shapes=[
            pltpu.VMEM((slots, block, GROUP * block), BF16),
            pltpu.VMEM((slots, GROUP * block, scenarios), BF16),
            pltpu.SemaphoreType.DMA((slots, 2, GROUP)),
        ],
        compiler_params=params(32),
        cost_estimate=pl.CostEstimate(
            flops=2 * coefficients.size * scenarios // parts, bytes_accessed=moved, transcendentals=0
        ),
        name="past",
    )(*(pltpu.with_memory_space_constraint(x, pltpu.HBM) for x in (todo, owner)), start, history, coefficients)


def scan_kernel(region, delays_ref, now_ref, now_group_ref, past_ref, past_group_ref):
    row_blocks, col_blocks = delays_ref.shape

    def look(k, found):
        found = list(found)
        delays = [[delays_ref[i, k * GROUP + g] for i in range(row_blocks)] for g in range(GROUP)]
        for g in range(GROUP):
            for i in range(row_blocks):
                delay = delays[g][i]
                here = jnp.where(delay == 0, 1, 0)
                now_ref[found[2 * i]] = k * GROUP + g
                past_ref[found[2 * i + 1]] = (k * GROUP + g) * 8 + delay - 1
                found[2 * i] += here
                found[2 * i + 1] += 1 - here
        return tuple(found)

    starts = tuple(jnp.int32(region * (n // 2)) for n in range(2 * row_blocks))
    found = lax.fori_loop(0, col_blocks // GROUP, look, starts)
    for n, (blocks, groups) in enumerate(((now_ref, now_group_ref), (past_ref, past_group_ref))):
        total = jnp.int32(0)
        for i in range(row_blocks):
            end = found[2 * i + n]
            for g in range(GROUP):
                blocks[end + g] = -1
            number = (end - region * i + (GROUP - 1)) // GROUP

            @pl.loop(0, number)
            def _(t):
                groups[total + t] = region * i + t * GROUP

            total = total + number
        groups[groups.shape[0] - 1] = total


def region_of(col_blocks):
    return 1 << (col_blocks + GROUP - 1).bit_length()


def scan(delays):
    row_blocks, col_blocks = delays.shape
    region = region_of(col_blocks)
    groups = row_blocks * (col_blocks // GROUP + 1)
    smem = pl.BlockSpec(memory_space=pltpu.SMEM)
    one = (jax.ShapeDtypeStruct((row_blocks * region,), I32), jax.ShapeDtypeStruct((groups + 1,), I32))
    return pl.pallas_call(
        functools.partial(scan_kernel, region),
        out_shape=one + one,
        in_specs=[smem],
        out_specs=(smem,) * 4,
        name="scan",
    )(delays)


def row_copies(pieces, rows, sems):
    part = pieces[0].shape[0]
    return [
        pltpu.make_async_copy(piece, rows.at[pl.ds(n * part, part)], sems.at[n]) for n, piece in enumerate(pieces)
    ]


def decode(head, mask_ref, first, blocks, sizes, skip, codes, rows):
    branch_rows = sizes[2]

    @pl.loop(0, blocks)
    def _(place):
        source = source_at(mask_ref, first, skip + place)
        at = (sizes[0] * CHAINS // LANES) % 8 + 1
        scales, _ = powers(exponent=head[source, at : at + 2, :])
        scales = scales * (1.0 / FULL)
        words = codes[pl.ds(pl.multiple_of((skip + place) * branch_rows, branch_rows), branch_rows), :]
        base = place * (4 * branch_rows)
        for side, part in enumerate((low_of(words), high_of(words))):
            value = part.astype(F32) * scales[side : side + 1, :]
            rows[pl.ds(base + side, branch_rows, stride=2), :] = value
            rows[pl.ds(base + 2 * branch_rows + side, branch_rows, stride=2), :] = -value


def scatter(sizes, first, skip, blocks, lists_ref, mask_ref, rows, acc):
    capacity, words, branch_rows = sizes
    bits = node_bits(acc[0].shape[0] // 2 - PAD)

    @pl.loop(0, blocks)
    def _(place):
        source = source_at(mask_ref, first, skip + place)
        base = place * (4 * branch_rows)
        start = source * words
        tally = start + CHAINS * capacity + lax.axis_index("col") * CHAINS
        most = lists_ref[tally]
        for chain in range(1, CHAINS):
            most = jnp.maximum(most, lists_ref[tally + chain])

        @pl.loop(0, (most + (UNROLL - 1)) // UNROLL)
        def _(j):
            for u in range(UNROLL):
                after = []
                for chain in range(CHAINS):
                    entry = lists_ref[start + chain * capacity + j * UNROLL + u]
                    row = pl.multiple_of(base + lax.shift_right_logical(entry, bits), 2)
                    at = pl.ds(pl.multiple_of(lax.bitwise_and(entry, (1 << bits) - 1), 2), 2)
                    after.append((acc[chain], at, acc[chain][at, :] + rows[pl.ds(row, 2), :]))
                for part, at, value in after:
                    part[at, :] = value


def head_copy(sizes, message_ref, head, sem):
    first = sizes[0] * CHAINS // LANES // 8 * 8
    return pltpu.make_async_copy(message_ref.at[:, pl.ds(first, head.shape[1])], head, sem)


def head_shape(sizes, devices):
    first = sizes[0] * CHAINS // LANES // 8 * 8
    return pltpu.VMEM((devices, sizes[1] // LANES - first, LANES), I32)


def add_ends(sizes, late, lists_ref, mask_ref, head, codes, rows, acc):
    branch_rows = sizes[2]
    first = late * (mask_ref.shape[1] // 2)
    blocks = codes.shape[0] // branch_rows
    batch = rows.shape[0] // (4 * branch_rows)
    for skip in range(0, blocks, batch):
        decode(head, mask_ref, first, batch, sizes, skip, codes, rows)
        scatter(sizes, first, skip, batch, lists_ref, mask_ref, rows, acc)


def early_kernel(sizes, flat_ref, mask_ref, message_ref, one_ref, two_ref, *more):
    acc, (codes, rows, head, lists_ref, sems) = more[:CHAINS], more[CHAINS:]
    copies = [
        *row_copies((one_ref, two_ref), codes, sems),
        head_copy(sizes, message_ref, head, sems.at[2]),
        pltpu.make_async_copy(flat_ref, lists_ref, sems.at[3]),
    ]
    for copy in copies:
        copy.start()
    clear = 512
    for part in acc:
        part[0 : 2 * PAD, :] = jnp.zeros((2 * PAD, LANES), F32)

        @pl.loop(0, part.shape[0] // clear)
        def _(n):
            part[pl.ds(pl.multiple_of(n * clear + 2 * PAD, 8), clear), :] = jnp.zeros((clear, LANES), F32)
    for copy in copies:
        copy.wait()
    add_ends(sizes, 0, lists_ref, mask_ref, head, codes, rows, acc)


def scatter_room(pieces, sizes, devices):
    rows = min(2 * pieces[0].shape[0], 16 * sizes[2])
    return [
        pltpu.VMEM((2 * pieces[0].shape[0], LANES), I32),
        pltpu.VMEM((4 * rows, LANES), F32),
        head_shape(sizes, devices),
        pltpu.SMEM((devices * sizes[1],), I32),
    ], (2 * pieces[0].shape[0] + 4 * rows + devices * 16) * LANES * 4 >> 20


def early_scatter(message, mask, pieces, nodes, sizes):
    room, mib = scatter_room(pieces, sizes, message.shape[0])
    smem = pl.BlockSpec(memory_space=pltpu.SMEM)
    hbm = pl.BlockSpec(memory_space=pl.ANY)
    return pl.pallas_call(
        functools.partial(early_kernel, sizes),
        out_shape=tuple(pltpu.VMEM((2 * (nodes // CHAINS + PAD), LANES), F32) for _ in range(CHAINS)),
        in_specs=[hbm, smem] + [hbm] * 3,
        out_specs=tuple(vmem(CHAINS)),
        scratch_shapes=[*room, pltpu.SemaphoreType.DMA((4,))],
        compiler_params=params(mib + 4),
        cost_estimate=pl.CostEstimate(flops=1 << 28, bytes_accessed=32 << 20, transcendentals=0),
        name="early",
    )(message.reshape(-1), mask, message, *pieces)


def now_kernel(
    block, slots, chunks, sizes,
    flat_ref, mask_ref, todo_ref, owner_ref, past_ref, message_ref,
    one_ref, two_ref, history_ref, coef_ref,
    charge_ref, out_ref, acc,
    codes, rows, head, lists_ref, charge, coef, source_of, total, row_sem, load_sem, store_sem, coef_sem,
):
    row_blocks, col_blocks = total.shape[0], charge.shape[0] // block
    copies = [
        *row_copies((one_ref, two_ref), codes, row_sem),
        head_copy(sizes, message_ref, head, row_sem.at[2]),
        pltpu.make_async_copy(flat_ref, lists_ref, row_sem.at[3]),
    ]
    for copy in copies:
        copy.start()
    load = pltpu.make_async_copy(history_ref.at[0], charge, load_sem)
    load.start()

    count = owner_ref[owner_ref.shape[0] - 1]
    region_bits = log2(region_of(col_blocks))

    def coef_copy(t, g):
        i = lax.shift_right_logical(owner_ref[t], region_bits)
        k = jnp.maximum(todo_ref[owner_ref[t] + g], 0)
        slot = lax.rem(t, slots)
        return pltpu.make_async_copy(
            coef_ref.at[pl.ds(pl.multiple_of(i * block, block), block),
                        pl.ds(pl.multiple_of(k * block, block), block)],
            coef.at[slot, :, pl.ds(g * block, block)],
            coef_sem.at[slot, g],
        )

    @pl.loop(0, jnp.minimum(count, slots))
    def _(t):
        for g in range(GROUP):
            coef_copy(t, g).start()

    for copy in copies:
        copy.wait()
    add_ends(sizes, 1, lists_ref, mask_ref, head, codes, rows, acc)
    load.wait()

    def store(k):
        at = pl.ds(pl.multiple_of(k * block, block), block)
        return pltpu.make_async_copy(charge.at[at], charge_ref.at[at], store_sem)

    @pl.loop(0, col_blocks // CHAINS)
    def _(group):
        for chain in range(CHAINS):
            k = group * CHAINS + chain
            at = pl.ds(pl.multiple_of(k * block, block), block)
            for side in range(2):
                lanes = slice(side * LANES, (side + 1) * LANES)
                held = pl.ds(group * (2 * block) + (2 * PAD + side), block, stride=2)
                charge[at, lanes] = (charge[at, lanes].astype(F32) + acc[chain][held, :]).astype(BF16)
            store(k).start()

    for i in range(row_blocks):
        total[i] = past_ref[i]

    @pl.loop(0, count)
    def _(t):
        for g in range(GROUP):
            k = todo_ref[owner_ref[t] + g]
            held = charge[pl.ds(pl.multiple_of(jnp.maximum(k, 0) * block, block), block), :]
            source_of[g * block : (g + 1) * block, :] = jnp.where(k >= 0, held, jnp.zeros_like(held))
        for g in range(GROUP):
            coef_copy(t, g).wait()
        slot = lax.rem(t, slots)
        total[lax.shift_right_logical(owner_ref[t], region_bits)] += jnp.dot(coef[slot], source_of[...], preferred_element_type=F32)

        @pl.when(t + slots < count)
        def _():
            for g in range(GROUP):
                coef_copy(t + slots, g).start()

    turned = jnp.concatenate([total[i].T for i in range(row_blocks)], axis=1)
    nodes = turned.shape[1]
    codes, head = coded_rows(turned)
    chunk = turned.shape[0] // chunks
    half = chunk // 2
    for c in range(chunks):
        one = slice(c * chunk, c * chunk + half)
        two = slice(c * chunk + half, (c + 1) * chunk)
        out_ref[c, :, :nodes] = pair(codes[one], codes[two])
        out_ref[c, :, nodes:] = both_heads(head[one], head[two])

    pltpu.make_async_copy(charge, charge_ref, store_sem).wait()


def now_product(message, mask, todo, owner, past, acc, pieces, history, coefficients, block, chunks, sizes):
    row_blocks, _, scenarios = past.shape
    rows = row_blocks * block
    nodes = history.shape[1]
    slots = 8
    smem = pl.BlockSpec(memory_space=pltpu.SMEM)
    hbm = pl.BlockSpec(memory_space=pl.ANY)
    held = [pltpu.with_memory_space_constraint(part, pltpu.VMEM) for part in acc]
    before, count = 10, len(acc)
    room, mib = scatter_room(pieces, sizes, message.shape[0])
    mib += (nodes * 2 + rows * 4 * 6) * scenarios + slots * GROUP * block * block * 2 >> 20

    def kernel(*refs):
        sums = refs[before + count + 2 : before + 2 * count + 2]
        ins, outs = refs[:before], refs[before + count : before + count + 2]
        now_kernel(block, slots, chunks, sizes, *ins, *outs, sums, *refs[before + 2 * count + 2 :])

    return pl.pallas_call(
        kernel,
        out_shape=(
            jax.ShapeDtypeStruct((nodes, scenarios), BF16),
            jax.ShapeDtypeStruct((chunks, scenarios // chunks // 2, rows + LANES), I32),
            *[pltpu.VMEM(part.shape, F32) for part in acc],
        ),
        in_specs=[hbm] + [smem] * 3 + vmem(1) + [hbm] * 5 + vmem(count),
        out_specs=(hbm, *vmem(1 + count)),
        input_output_aliases={before + n: 2 + n for n in range(count)},
        scratch_shapes=[
            *room,
            pltpu.VMEM((nodes, scenarios), BF16),
            pltpu.VMEM((slots, block, GROUP * block), BF16),
            pltpu.VMEM((GROUP * block, scenarios), BF16),
            pltpu.VMEM((row_blocks, block, scenarios), F32),
            pltpu.SemaphoreType.DMA((4,)),
            pltpu.SemaphoreType.DMA,
            pltpu.SemaphoreType.DMA,
            pltpu.SemaphoreType.DMA((slots, GROUP)),
        ],
        compiler_params=params(mib + 6),
        cost_estimate=pl.CostEstimate(flops=1 << 30, bytes_accessed=80 << 20, transcendentals=0),
        name="now",
    )(message.reshape(-1), mask, todo, owner, past, message, *pieces, history, coefficients, *held)[:2]


def sum_kernel(got_ref, out_ref):
    sources, half, width = got_ref.shape
    nodes = width - LANES
    codes, heads = [], []
    for side in range(2):
        total = jnp.zeros((half, nodes), F32)
        for source in range(sources):
            words = got_ref[source, :, :nodes]
            scale, mean = scale_and_mean(got_ref[source, :, nodes:], side)
            total = total + ((high_of(words) if side else low_of(words)).astype(F32) * scale + mean)
        code, head = coded_rows(total)
        codes.append(code)
        heads.append(head)
    out_ref[:, :nodes] = pair(*codes)
    out_ref[:, nodes:] = both_heads(*heads)


def sum_columns(got):
    return pl.pallas_call(
        sum_kernel,
        out_shape=jax.ShapeDtypeStruct(got.shape[1:], I32),
        in_specs=vmem(1),
        out_specs=vmem()[0],
        compiler_params=params(16),
        name="sum",
    )(got)


def drop_kernel(node_ref, word_ref, out_ref):
    row_count, half, width = word_ref.shape
    nodes = width - LANES
    per_row = nodes // LANES
    worth = [[scale_and_mean(word_ref[r, :, nodes:], side) for side in range(2)] for r in range(row_count)]

    @pl.loop(0, node_ref.shape[1] // LANES)
    def _(group):
        at = pl.ds(pl.multiple_of(group * LANES, LANES), LANES)
        found = []
        for end in range(2):
            node = jnp.broadcast_to(node_ref[pl.ds(end, 1), at], (8, LANES))
            inner = lax.bitwise_and(node, LANES - 1)
            outer = lax.shift_right_logical(node, log2(LANES))
            row = lax.shift_right_logical(node, log2(nodes))
            for e in range(0, half, 8):
                values = [jnp.zeros((8, LANES), F32)] * 2
                for r in range(row_count):
                    word = jnp.zeros((8, LANES), I32)
                    for h in range(per_row):
                        held = word_ref[r, e : e + 8, h * LANES : (h + 1) * LANES]
                        seen = jnp.take_along_axis(held, inner, axis=1, mode="promise_in_bounds")
                        word = jnp.where(outer == r * per_row + h, seen, word)
                    for side, code in enumerate((low_of(word), high_of(word))):
                        scale, mean = worth[r][side]
                        value = code.astype(F32) * scale[e : e + 8] + mean[e : e + 8]
                        values[side] = jnp.where(row == r, value, values[side])
                found.append(values)
        groups = len(found) // 2
        for e in range(groups):
            for side in range(2):
                rows = pl.ds(side * half + e * 8, 8)
                out_ref[rows, at] = found[e][side] - found[groups + e][side]


def row_drops(nodes, words):
    return pl.pallas_call(
        drop_kernel,
        out_shape=jax.ShapeDtypeStruct((2 * words.shape[1], nodes.shape[1]), F32),
        in_specs=vmem(2),
        out_specs=vmem()[0],
        compiler_params=params(24),
        name="drops",
    )(nodes, words)


def branch_lists(index, owner, slot, slab_owner, slab_offset, col_count, share, sizes):
    lists, tally, slab = make_lists(owner, slot, slab_owner, slab_offset, share, sizes, col_count * CHAINS)
    slab = slab.reshape(-1, LANES)
    return lists.reshape(col_count, -1, LANES), tally, jnp.concatenate([index, slab], axis=0)


def share_lists(lists, tally, slab, row_count, col_count):
    common = jnp.concatenate([tally, slab], axis=0)
    extra = -(lists.shape[1] + common.shape[0]) % 8
    common = jnp.concatenate([common, jnp.zeros((extra, LANES), I32)], axis=0)
    common = jnp.broadcast_to(common[None], (col_count, *common.shape))
    message = jnp.concatenate([lists, common], axis=1)
    message = jnp.broadcast_to(message[None], (row_count, *message.shape)).reshape(-1, LANES)
    return lax.all_to_all(message, ALL, split_axis=0, concat_axis=0, tiled=True)


def local(currents, branch_owner, branch_slot, history, coefficients, delays, slab_owner, slab_offset):
    row_count = lax.axis_size("row")
    col_count = lax.axis_size("col")
    devices = row_count * col_count
    branch_rows, scenarios = currents.shape
    owned = history.shape[1] // row_count
    block = coefficients.shape[1] // delays.shape[1]
    per_owner = 8 * branch_rows // devices
    capacity = -(-min(2 * branch_rows, row_count * per_owner) // LANES) * LANES
    chain_rows = history.shape[1] // CHAINS
    share = coefficients.shape[0] * row_count // devices
    my_row, my_col = lax.axis_index("row"), lax.axis_index("col")
    me = my_row * col_count + my_col
    pairs, sibling = gather_steps(row_count, col_count)
    parts = 2
    past = jnp.zeros((delays.shape[0], block, scenarios), F32)
    together = lax.optimization_barrier

    def add_past(past, part):
        return past_product(late, late_owner, coefficients, history, past, block, part, parts)

    held, index = pack(currents)
    jobs = {1: (0,), 2: (1,)}
    message = None
    for number, step in enumerate(pairs[:-1]):
        held, past = together((held, past))
        got = lax.ppermute(held, ALL, step)
        for job in jobs.get(number, ()):
            past = add_past(past, job)
        if number == 0:
            lists, tally, slab = branch_lists(
                index, branch_owner, branch_slot, slab_owner, slab_offset, col_count, share,
                (row_count, owned, block, capacity, chain_rows),
            )
            todo, owner, late, late_owner = scan(delays)
            got, past, lists, tally, slab, late = together((got, past, lists, tally, slab, late))
            message = share_lists(lists, tally, slab, row_count, col_count)
        elif number == len(pairs) - 2:
            got, past, message = together((got, past, message))
        else:
            got, past = together((got, past))
        held = jnp.concatenate([held, got], axis=0)
    held, past = together((held, past))
    mid = lax.ppermute(held, ALL, pairs[-1])
    far = lax.ppermute(held, ALL, sibling)

    list_tiles = CHAINS * capacity // LANES
    slab_rows = slab_owner.shape[0]
    slab_tiles = 2 * slab_rows // LANES
    width = message.shape[0] // devices
    message = message.reshape(devices, width, LANES)
    row_slab = lax.dynamic_slice_in_dim(message, my_row * col_count, col_count, 0)
    row_slab = row_slab[:, list_tiles + 3 : list_tiles + 3 + slab_tiles]
    row_slab = row_slab.reshape(col_count, 2, slab_rows).transpose(1, 0, 2).reshape(2, col_count * slab_rows)

    mask = mask_table(row_count, col_count)
    sizes = (capacity, width * LANES, branch_rows)
    acc = early_scatter(message, mask, (held, far), history.shape[1], sizes)
    mid, past, acc = together((mid, past, acc))
    last = lax.ppermute(mid, ALL, sibling)
    charge, partial = now_product(
        message, mask, todo, owner, past, acc, (mid, last), history, coefficients,
        block, col_count, sizes,
    )

    got = lax.all_to_all(partial, "col", split_axis=0, concat_axis=0, tiled=True)
    mine = sum_columns(got)
    potentials = lax.all_gather(mine, "row", axis=0, tiled=False)
    found = row_drops(row_slab, potentials)
    excitations = found.shape[0]
    found = found.reshape(excitations, col_count, slab_rows).transpose(1, 0, 2)
    found = lax.all_to_all(found, "col", split_axis=0, concat_axis=0, tiled=True)
    return charge, found.reshape(col_count * excitations, slab_rows).T


def solution(mesh):
    both = P(("row", "col"), None)
    placed = (both, both, both, P(None, "col", None), P("row", "col"), P("row", "col"), both, both)
    return jax.shard_map(
        local,
        mesh=mesh,
        in_specs=placed,
        out_specs=(P("col", None), both),
        check_vma=False,
    )
```
